32 devices in a mesh: pb: 8 (over y, x, core), kv: 4 (over z).
Axes of the slice: x: 2, y: 2, z: 4, core: 2. Of those that a mesh axis runs over, the one named last changes fastest.
Arguments:
- queries: float32 [4096, 256], P(('pb', 'kv')), may hold values from -200 to 200
- keys: float32 [4096, 256], P(('pb', 'kv')), may hold values from -8 to 8
- values: float32 [4096, 256], P(('pb', 'kv')), may hold values from -192 to 192
- query_tangent: float32 [4096, 256], P(('pb', 'kv')), may hold values from -6 to 6
- key_tangent: float32 [4096, 256], P(('pb', 'kv')), may hold values from -6 to 6
- value_tangent: float32 [4096, 256], P(('pb', 'kv')), may hold values from -192 to 192
Outputs:
- attended: float32 [4096, 256], P(('pb', 'kv'))
- attended_tangent: float32 [4096, 256], P(('pb', 'kv'))
The draws below stay inside these ranges and needn't reach their ends.
All inputs are finite; a program needn't handle non-finite values.
Results may differ from the reference program's by a relative error of at most 0.0003.
Values sent between devices are 32-bit elements; how exact they have to be, the bound alone decides.
No kernel may reach another device: no remote copies, remote signals or barrier semaphores. Data moves between devices by JAX's collectives and lax.ppermute only.
A program may use at most 128 MiB of HBM per device.

```python
import math
import jax
import jax.numpy as jnp
from jax import lax

DH = 128
HEADS = 2
WIDTH = 256
SEQ = 4096


def drawn_pair(key):
    shape = (SEQ, HEADS, DH)
    keys = jnp.clip(jax.random.normal(jax.random.fold_in(key, 11), shape, jnp.float32), -6.0, 6.0) * 1.2
    queries = jnp.clip(jax.random.normal(jax.random.fold_in(key, 12), shape, jnp.float32), -6.0, 6.0) * 1.2
    row_scale = jnp.exp(jax.random.uniform(jax.random.fold_in(key, 16), (SEQ, HEADS, 1), jnp.float32, 0.0, math.log(16.0)))
    queries = queries * row_scale
    return (queries.reshape(SEQ, HEADS * DH), keys.reshape(SEQ, HEADS * DH))


def draw_queries(key, part):
    return drawn_pair(key)[0]


def draw_keys(key, part):
    return drawn_pair(key)[1]


def level_of(rng, extent, split, smallest, high):
    factor_of, own = 1.0, jax.random.fold_in(rng, 6)
    for dim, shards_of in split:
        heights = jnp.exp(jax.random.uniform(jax.random.fold_in(own, dim), (shards_of,), jnp.float32, smallest / len(split), high / len(split)))
        factor_of = factor_of * jnp.repeat(heights, extent[dim] // shards_of).reshape([-1 if axis == dim else 1 for axis in range(len(extent))])
    return factor_of


def bell_draw(rng, dims, spread, reach, shards=(), held_as=jnp.bfloat16):
    result = spread * jax.random.normal(rng, dims, jnp.float32)
    if shards:
        result = result * level_of(rng, dims, shards, -0.22, 0.18)
    return jnp.clip(result, -reach, reach).astype(held_as)


def setup_inputs(seed: int = 0) -> dict:
    streams_of = jax.random.split(jax.random.key(seed), 7)
    return {
        "queries": draw_queries(jax.random.fold_in(streams_of[6], 71), 0),
        "keys": draw_keys(jax.random.fold_in(streams_of[6], 71), 0),
        "values": bell_draw(streams_of[2], (SEQ, WIDTH), 32.0, 192.0, ((0, 32),), jnp.float32),
        "query_tangent": bell_draw(streams_of[3], (SEQ, WIDTH), 1.0, 6.0, ((0, 32),), jnp.float32),
        "key_tangent": bell_draw(streams_of[4], (SEQ, WIDTH), 1.0, 6.0, ((0, 32),), jnp.float32),
        "value_tangent": bell_draw(streams_of[5], (SEQ, WIDTH), 32.0, 192.0, ((0, 32),), jnp.float32),
    }


def cross(left, right):
    return lax.dot_general(left, right, (((1,), (1,)), ((), ())), precision=lax.Precision.HIGHEST, preferred_element_type=jnp.float32)

def product(left, right):
    return jnp.dot(left, right, precision=lax.Precision.HIGHEST, preferred_element_type=jnp.float32)

def reference(queries, keys, values, query_tangent, key_tangent, value_tangent):
    total = queries.shape[0]
    block = min(1024, total)
    heads = queries.shape[1] // DH
    scale = 1.0 / math.sqrt(DH)
    outs = []
    tangents = []
    for head in range(heads):
        cols = slice(head * DH, (head + 1) * DH)
        key_h = keys[:, cols]
        val_h = values[:, cols]
        dkey_h = key_tangent[:, cols]
        dval_h = value_tangent[:, cols]
        q_blocks = queries[:, cols].reshape(total // block, block, DH)
        dq_blocks = query_tangent[:, cols].reshape(total // block, block, DH)

        def one_block(pair):
            q_rows, dq_rows = pair
            scores = cross(q_rows, key_h) * scale
            score_tangent = (cross(dq_rows, key_h) + cross(q_rows, dkey_h)) * scale
            peak = lax.optimization_barrier(jnp.max(scores, axis=1, keepdims=True))
            expo = jnp.exp(scores - peak)
            weights = expo / lax.optimization_barrier(jnp.sum(expo, axis=1, keepdims=True))
            mean_t = lax.optimization_barrier(jnp.sum(weights * score_tangent, axis=1, keepdims=True))
            attended = product(weights, val_h)
            tangent = product(weights * (score_tangent - mean_t), val_h) + product(weights, dval_h)
            return (attended, tangent)
        att, tan = lax.map(one_block, (q_blocks, dq_blocks))
        outs.append(att.reshape(total, DH))
        tangents.append(tan.reshape(total, DH))
    return (jnp.concatenate(outs, axis=1), jnp.concatenate(tangents, axis=1))
```

```python
import functools
import math

import jax
import jax.numpy as jnp
from jax import lax
from jax.experimental import pallas as pl
from jax.experimental.pallas import tpu as pltpu
from jax.sharding import PartitionSpec as P

DH = 128
LOG2E = 1.4426950408889634
STAT_ROWS = 8
VMEM_LIMIT = 56 * 1024 * 1024


def split2(x):
    high = x.astype(jnp.bfloat16)
    return high, (x - high.astype(jnp.float32)).astype(jnp.bfloat16)


def split3(x):
    high = x.astype(jnp.bfloat16)
    rest = x - high.astype(jnp.float32)
    mid = rest.astype(jnp.bfloat16)
    return high, mid, (rest - mid.astype(jnp.float32)).astype(jnp.bfloat16)


def dot_nt(left, right):
    return lax.dot_general(
        left, right, (((1,), (1,)), ((), ())), preferred_element_type=jnp.float32
    )


def dot_nn(left, right):
    return jnp.dot(left, right, preferred_element_type=jnp.float32)


def attend_kernel(heads, n_q, n_k, rows, tile_blocks, *refs):
    q_refs = refs[:n_q]
    k_refs = refs[n_q : n_q + n_k]
    out_refs = refs[n_q + n_k : n_q + n_k + n_q]
    qa, qb, ka, kb, va, vb, vc = refs[n_q + n_k + n_q :]
    width = heads * DH
    scale = 1.0 / math.sqrt(DH)
    stats = [[] for _ in range(n_q)]
    for head in range(heads):
        c0, c1 = head * DH, width + head * DH
        c2, c3 = 2 * width + head * DH, 3 * width + head * DH
        for b, ref in enumerate(q_refs):
            at = slice(b * rows, (b + 1) * rows)
            q = ref[:, c0 : c0 + DH]
            dq = ref[:, c1 : c1 + DH]
            a1, a2, a3 = split3(q * (scale * LOG2E))
            qa[at, :] = jnp.concatenate([a1, a1, a2, a1, a3, a2], axis=1)
            q1, q2 = split2(q * scale)
            d1, d2 = split2(dq * scale)
            qb[at, :] = jnp.concatenate([d1, q1, d1, q1, d2, q2], axis=1)
        for b, ref in enumerate(k_refs):
            at = slice(b * rows, (b + 1) * rows)
            k1, k2, k3 = split3(ref[:, c0 : c0 + DH])
            d1, d2 = split2(ref[:, c1 : c1 + DH])
            v1, v2 = split2(ref[:, c2 : c2 + DH])
            w1, w2 = split2(ref[:, c3 : c3 + DH])
            ka[at, :] = jnp.concatenate([k1, k2, k1, k3, k1, k2], axis=1)
            kb[at, :] = jnp.concatenate([k1, d1, k2, d2, k1, d1], axis=1)
            va[at, :] = jnp.concatenate([v1, w1], axis=1)
            vb[at, :] = jnp.concatenate([v2, w2], axis=1)
            vc[at, :] = jnp.concatenate([v1, v2], axis=1)
        for t in range(n_q // tile_blocks):
            at = slice(t * tile_blocks * rows, (t + 1) * tile_blocks * rows)
            s = dot_nt(qa[at, :], ka[...])
            st = dot_nt(qb[at, :], kb[...])
            peak = jnp.max(s, axis=1, keepdims=True)
            e = jnp.exp2(s - peak)
            w = e * st
            total = jnp.sum(e, axis=1, keepdims=True)
            total_t = jnp.sum(w, axis=1, keepdims=True)
            e1, e2 = split2(e)
            w1, w2 = split2(w)
            both = dot_nn(e1, va[...]) + dot_nn(e1, vb[...]) + dot_nn(e2, va[...])
            first = dot_nn(w1, vc[...])
            numer = both[:, :DH]
            numer_t = both[:, DH:] + first[:, :DH] + first[:, DH:] + dot_nn(w2, vc[:, :DH])
            for i in range(tile_blocks):
                b = t * tile_blocks + i
                part = slice(i * rows, (i + 1) * rows)
                out_refs[b][0:rows, c0 : c0 + DH] = numer[part]
                out_refs[b][0:rows, c1 : c1 + DH] = numer_t[part]
                stats[b] += [peak[part], total[part], total_t[part]]
    lane = lax.broadcasted_iota(jnp.int32, (rows, DH), 1)
    for b in range(n_q):
        wide = jnp.zeros((rows, DH), jnp.float32)
        for i, column in enumerate(stats[b]):
            wide = jnp.where(lane == i, column, wide)
        out_refs[b][rows : rows + STAT_ROWS, :] = jnp.zeros((STAT_ROWS, 2 * width), jnp.float32)
        out_refs[b][rows : rows + STAT_ROWS, 0:rows] = wide.T[0:STAT_ROWS, :]


def finish_kernel(heads, n_q, rows, *refs):
    part_refs = refs[:n_q]
    out_ref, tan_ref = refs[n_q:]
    width = heads * DH
    wides = [
        jnp.concatenate(
            [ref[rows : rows + STAT_ROWS, 0:rows], jnp.zeros((DH - STAT_ROWS, rows), jnp.float32)], axis=0
        ).T
        for ref in part_refs
    ]
    for head in range(heads):
        c0, c1 = head * DH, width + head * DH
        peaks = [wide[:, 3 * head : 3 * head + 1] for wide in wides]
        top = functools.reduce(jnp.maximum, peaks)
        total = total_t = numer = numer_t = 0.0
        for ref, wide, peak in zip(part_refs, wides, peaks):
            factor = jnp.exp2(peak - top)
            total += factor * wide[:, 3 * head + 1 : 3 * head + 2]
            total_t += factor * wide[:, 3 * head + 2 : 3 * head + 3]
            numer += factor * ref[0:rows, c0 : c0 + DH]
            numer_t += factor * ref[0:rows, c1 : c1 + DH]
        attended = numer / total
        out_ref[:, c0 : c0 + DH] = attended
        tan_ref[:, c0 : c0 + DH] = (numer_t - attended * total_t) / total


def swap(x, axis, size, mask):
    return lax.ppermute(x, axis, [(i, i ^ mask) for i in range(size)])


def per_device(n_pb, n_kv, queries, keys, values, query_tangent, key_tangent, value_tangent):
    rows, width = queries.shape
    heads = width // DH
    mine_q = jnp.concatenate([queries, query_tangent], axis=1)
    mine_k = jnp.concatenate([keys, key_tangent, values, value_tangent], axis=1)
    k_blocks = [mine_k] + [swap(mine_k, "pb", n_pb, m) for m in range(2, n_pb, 2)]
    q_blocks = [mine_q] + [swap(mine_q, "kv", n_kv, m) for m in range(1, n_kv)]
    k_blocks = k_blocks + [swap(x, "pb", n_pb, 1) for x in k_blocks]
    n_q, n_k = len(q_blocks), len(k_blocks)
    total_q, total_k = n_q * rows, n_k * rows
    bf16 = jnp.bfloat16
    parts = pl.pallas_call(
        functools.partial(attend_kernel, heads, n_q, n_k, rows, 2),
        out_shape=[jax.ShapeDtypeStruct((rows + STAT_ROWS, 2 * width), jnp.float32)] * n_q,
        scratch_shapes=[
            pltpu.VMEM((total_q, 6 * DH), bf16),
            pltpu.VMEM((total_q, 6 * DH), bf16),
            pltpu.VMEM((total_k, 6 * DH), bf16),
            pltpu.VMEM((total_k, 6 * DH), bf16),
            pltpu.VMEM((total_k, 2 * DH), bf16),
            pltpu.VMEM((total_k, 2 * DH), bf16),
            pltpu.VMEM((total_k, 2 * DH), bf16),
        ],
        compiler_params=pltpu.CompilerParams(vmem_limit_bytes=VMEM_LIMIT),
    )(*q_blocks, *k_blocks)
    back = [parts[0]] + [swap(parts[m], "kv", n_kv, m) for m in range(1, n_kv)]
    return tuple(
        pl.pallas_call(
            functools.partial(finish_kernel, heads, n_q, rows),
            out_shape=[jax.ShapeDtypeStruct((rows, width), jnp.float32)] * 2,
            compiler_params=pltpu.CompilerParams(vmem_limit_bytes=VMEM_LIMIT),
        )(*back)
    )


def solution(mesh):
    spec = P(("pb", "kv"), None)
    body = functools.partial(per_device, mesh.shape["pb"], mesh.shape["kv"])
    return jax.shard_map(body, mesh=mesh, in_specs=(spec,) * 6, out_specs=(spec,) * 2, check_vma=False)
```

```python
import functools
import math

import jax
import jax.numpy as jnp
from jax import lax
from jax.experimental import pallas as pl
from jax.experimental.pallas import tpu as pltpu
from jax.sharding import PartitionSpec as P

DH = 128
LOG2E = 1.4426950408889634
STAT_ROWS = 8
AXES = ("pb", "kv")
PARAMS = pltpu.CompilerParams(vmem_limit_bytes=56 * 1024 * 1024)


def split2(x):
    high = x.astype(jnp.bfloat16)
    return high, (x - high.astype(jnp.float32)).astype(jnp.bfloat16)


def split3(x):
    high = x.astype(jnp.bfloat16)
    rest = x - high.astype(jnp.float32)
    mid = rest.astype(jnp.bfloat16)
    return high, mid, (rest - mid.astype(jnp.float32)).astype(jnp.bfloat16)


def dot_nt(left, right):
    return lax.dot_general(
        left, right, (((1,), (1,)), ((), ())), preferred_element_type=jnp.float32
    )


def dot_nn(left, right):
    return jnp.dot(left, right, preferred_element_type=jnp.float32)


def f32(*shape):
    return jax.ShapeDtypeStruct(shape, jnp.float32)


def give_kernel(core_ref, *refs):
    *ins, out = refs
    column = pl.multiple_of((1 - core_ref[0]) * DH, DH)
    for i, ref in enumerate(ins):
        out[:, i * DH : (i + 1) * DH] = ref[:, pl.ds(column, DH)]


def join_kernel(core_ref, *refs):
    *ins, got, out_q, out_k = refs
    rows = got.shape[0]
    column = pl.multiple_of(core_ref[0] * DH, DH)
    for i, ref in enumerate(ins):
        out, at = (out_q, i) if i < 2 else (out_k, i - 2)
        out[0:rows, at * DH : (at + 1) * DH] = ref[:, pl.ds(column, DH)]
    out_q[rows:, :] = got[:, 0 : 2 * DH]
    out_k[rows:, :] = got[:, 2 * DH :]


def attend_kernel(n_q, n_k, rows, has_prev, last, *refs):
    refs = list(refs)

    def take(count):
        head, refs[:] = refs[:count], refs[count:]
        return head

    q_refs, k_refs = take(n_q), take(n_k)
    prev = take(2 * n_q) if has_prev else None
    outs = take(n_q if last else 2 * n_q)
    ka, kb, va, vb, vc = refs
    scale = 1.0 / math.sqrt(DH)
    for b, ref in enumerate(k_refs):
        at = slice(b * rows, (b + 1) * rows)
        k1, k2, k3 = split3(ref[:, 0:DH])
        d1, d2 = split2(ref[:, DH : 2 * DH])
        v1, v2 = split2(ref[:, 2 * DH : 3 * DH])
        w1, w2 = split2(ref[:, 3 * DH : 4 * DH])
        ka[at, :] = jnp.concatenate([k1, k2, k1, k3, k1, k2], axis=1)
        kb[at, :] = jnp.concatenate([k1, d1, k2, d2, k1, d1], axis=1)
        va[at, :] = jnp.concatenate([v1, w1], axis=1)
        vb[at, :] = jnp.concatenate([v2, w2], axis=1)
        vc[at, :] = jnp.concatenate([v1, v2], axis=1)
    lane = lax.broadcasted_iota(jnp.int32, (rows, DH), 1)
    for b, ref in enumerate(q_refs):
        q = ref[:, 0:DH]
        a1, a2, a3 = split3(q * (scale * LOG2E))
        q1, q2 = split2(q * scale)
        d1, d2 = split2(ref[:, DH : 2 * DH] * scale)
        s = dot_nt(jnp.concatenate([a1, a1, a2, a1, a3, a2], axis=1), ka[...])
        st = dot_nt(jnp.concatenate([d1, q1, d1, q1, d2, q2], axis=1), kb[...])
        peak = jnp.max(s, axis=1, keepdims=True)
        if has_prev:
            old = prev[2 * b + 1][:, 0:3]
            peak = jnp.maximum(peak, old[:, 0:1])
        e = jnp.exp2(s - peak)
        w = e * st
        total = jnp.sum(e, axis=1, keepdims=True)
        total_t = jnp.sum(w, axis=1, keepdims=True)
        e1, e2 = split2(e)
        w1, w2 = split2(w)
        both = dot_nn(e1, va[...]) + dot_nn(e1, vb[...]) + dot_nn(e2, va[...])
        first = dot_nn(w1, vc[...])
        numer = both[:, :DH]
        numer_t = both[:, DH:] + first[:, :DH] + first[:, DH:] + dot_nn(w2, vc[:, :DH])
        if has_prev:
            factor = jnp.exp2(old[:, 0:1] - peak)
            total += factor * old[:, 1:2]
            total_t += factor * old[:, 2:3]
            numer += factor * prev[2 * b][:, :DH]
            numer_t += factor * prev[2 * b][:, DH:]
        stats = jnp.where(lane == 0, peak, jnp.where(lane == 1, total, total_t))
        if last:
            outs[b][0:rows, :DH] = numer
            outs[b][0:rows, DH:] = numer_t
            outs[b][rows:, :] = stats.T[0:STAT_ROWS, :]
        else:
            outs[2 * b][:, :DH] = numer
            outs[2 * b][:, DH:] = numer_t
            outs[2 * b + 1][...] = stats


def attend(q_blocks, k_blocks, prev, last):
    n_q, n_k, rows = len(q_blocks), len(k_blocks), q_blocks[0].shape[0]
    assert rows == 2 * DH
    keys = n_k * rows
    if last:
        shapes = [f32(rows + STAT_ROWS, 2 * DH)] * n_q
    else:
        shapes = [f32(rows, 2 * DH), f32(rows, DH)] * n_q
    work = n_q * rows * keys
    return pl.pallas_call(
        functools.partial(attend_kernel, n_q, n_k, rows, bool(prev), last),
        out_shape=shapes,
        scratch_shapes=[pltpu.VMEM((keys, w * DH), jnp.bfloat16) for w in (6, 6, 2, 2, 2)],
        compiler_params=PARAMS,
        cost_estimate=pl.CostEstimate(
            flops=work * 2 * 256 * 18, transcendentals=work, bytes_accessed=n_q * rows * 4096 + keys * 2048
        ),
    )(*q_blocks, *k_blocks, *prev)


def finish_kernel(n_q, rows, *refs):
    part_refs = refs[:n_q]
    keep, give = refs[n_q:]
    half = rows // 2
    wides = [
        jnp.concatenate(
            [ref[rows:, :], jnp.zeros((DH - STAT_ROWS, rows), jnp.float32)], axis=0
        ).T
        for ref in part_refs
    ]
    peaks = [wide[:, 0:1] for wide in wides]
    top = functools.reduce(jnp.maximum, peaks)
    total = total_t = numer = numer_t = 0.0
    for ref, wide, peak in zip(part_refs, wides, peaks):
        factor = jnp.exp2(peak - top)
        total += factor * wide[:, 1:2]
        total_t += factor * wide[:, 2:3]
        numer += factor * ref[0:rows, :DH]
        numer_t += factor * ref[0:rows, DH:]
    attended = numer / total
    tangent = (numer_t - attended * total_t) / total
    for ref, at in ((keep, slice(0, half)), (give, slice(half, rows))):
        ref[:, :DH] = attended[at]
        ref[:, DH:] = tangent[at]


def place_kernel(core_ref, keep, got, out, tan):
    for ref, core in ((keep, core_ref[0]), (got, 1 - core_ref[0])):
        column = pl.multiple_of(core * DH, DH)
        out[:, pl.ds(column, DH)] = ref[:, :DH]
        tan[:, pl.ds(column, DH)] = ref[:, DH:]


def bits_of(n_pb, n_kv):
    low = n_kv.bit_length() - 1
    far = [1 << i for i in range(low)]
    near = [1 << (low + i) for i in range(1, n_pb.bit_length() - 1)]
    one = far[0::2] + near[1::2]
    two = far[1::2] + near[0::2]
    return ((one, two), (two, one)) if len(one) == len(two) else ((one, one), (two, two))


def per_device(n_pb, n_kv, *arrays):
    rows, width = arrays[0].shape
    assert width == 2 * DH and n_pb & (n_pb - 1) == 0 and n_kv & (n_kv - 1) == 0
    q_bits, k_bits = bits_of(n_pb, n_kv)
    core = (lax.axis_index("pb") % 2).astype(jnp.int32).reshape(1)

    def swap(x, masks):
        return lax.ppermute(
            x, AXES, [(i, i ^ masks[i // n_kv % 2]) for i in range(n_pb * n_kv)]
        )

    smem = pl.BlockSpec(memory_space=pltpu.SMEM)
    vmem = pl.BlockSpec(memory_space=pltpu.VMEM)
    order = (0, 3, 1, 4, 2, 5)
    arrays = [arrays[i] for i in order]
    give = pl.pallas_call(
        give_kernel,
        out_shape=f32(rows, 6 * DH),
        in_specs=[smem] + [vmem] * 6,
        compiler_params=PARAMS,
    )(core, *arrays)
    got = swap(give, (n_kv, n_kv))
    mine_q, mine_k = pl.pallas_call(
        join_kernel,
        out_shape=[f32(2 * rows, 2 * DH), f32(2 * rows, 4 * DH)],
        in_specs=[smem] + [vmem] * 7,
        compiler_params=PARAMS,
    )(core, *arrays, got)

    q_blocks, k_blocks = [mine_q], [mine_k]
    for one, two in zip(*k_bits):
        k_blocks += [swap(x, (one, two)) for x in k_blocks]
    for one, two in zip(*q_bits):
        q_blocks += [swap(x, (one, two)) for x in q_blocks]
    n_q = len(q_blocks)
    states = attend(q_blocks, k_blocks[0::2], [], False)
    parts = [None] * n_q
    for start in (1, 0):
        which = list(range(start, n_q, 2))
        prev = [states[2 * b + i] for b in which for i in range(2)]
        for b, part in zip(which, attend([q_blocks[b] for b in which], k_blocks[1::2], prev, True)):
            parts[b] = part

    def mask(bits, index):
        return sum(bit for i, bit in enumerate(bits) if index >> i & 1)

    back = [parts[0]] + [
        swap(parts[b], (mask(q_bits[0], b), mask(q_bits[1], b))) for b in range(n_q - 1, 0, -1)
    ]
    keep, give = pl.pallas_call(
        functools.partial(finish_kernel, n_q, 2 * rows),
        out_shape=[f32(rows, 2 * DH)] * 2,
        compiler_params=PARAMS,
    )(*back)
    got = swap(give, (n_kv, n_kv))
    return tuple(
        pl.pallas_call(
            place_kernel,
            out_shape=[f32(rows, width)] * 2,
            in_specs=[smem, vmem, vmem],
            compiler_params=PARAMS,
        )(core, keep, got)
    )


def solution(mesh):
    spec = P(AXES, None)
    body = functools.partial(per_device, mesh.shape["pb"], mesh.shape["kv"])
    return jax.shard_map(body, mesh=mesh, in_specs=(spec,) * 6, out_specs=(spec,) * 2, check_vma=False)
```

```python
import functools
import math

import jax
import jax.numpy as jnp
from jax import lax
from jax.experimental import pallas as pl
from jax.experimental.pallas import tpu as pltpu
from jax.sharding import PartitionSpec as P

DH = 128
LOG2E = 1.4426950408889634
STAT_ROWS = 8
AXES = ("pb", "kv")


def params(mib):
    return pltpu.CompilerParams(vmem_limit_bytes=mib * 1024 * 1024)


def split2(x):
    high = x.astype(jnp.bfloat16)
    return high, (x - high.astype(jnp.float32)).astype(jnp.bfloat16)


def split3(x):
    high = x.astype(jnp.bfloat16)
    rest = x - high.astype(jnp.float32)
    mid = rest.astype(jnp.bfloat16)
    return high, mid, (rest - mid.astype(jnp.float32)).astype(jnp.bfloat16)


def dot_nt(left, right):
    return lax.dot_general(
        left, right, (((1,), (1,)), ((), ())), preferred_element_type=jnp.float32
    )


def dot_nn(left, right):
    return jnp.dot(left, right, preferred_element_type=jnp.float32)


def f32(*shape):
    return jax.ShapeDtypeStruct(shape, jnp.float32)


def pack_kernel(core_ref, *refs):
    *ins, own_q, own_k, give, give_k = refs
    own = pl.multiple_of(core_ref[0] * DH, DH)
    other = pl.multiple_of((1 - core_ref[0]) * DH, DH)
    for i, ref in enumerate(ins):
        out, at = (own_q, i) if i < 2 else (own_k, i - 2)
        out[:, at * DH : (at + 1) * DH] = ref[:, pl.ds(own, DH)]
        far = ref[:, pl.ds(other, DH)]
        give[:, i * DH : (i + 1) * DH] = far
        if i >= 2:
            give_k[:, at * DH : (at + 1) * DH] = far


def join_kernel(own_q, own_k, got, out_q, out_k):
    rows = got.shape[0]
    out_q[0:rows, :] = own_q[...]
    out_q[rows:, :] = got[:, 0 : 2 * DH]
    out_k[0:rows, :] = own_k[...]
    out_k[rows:, :] = got[:, 2 * DH :]


def attend_kernel(n_q, n_k, rows, has_prev, last, *refs):
    refs = list(refs)

    def take(count):
        head, refs[:] = refs[:count], refs[count:]
        return head

    q_refs, k_refs = take(n_q), take(n_k)
    prev = take(2 * n_q) if has_prev else None
    outs = take(2 * n_q)
    ka, kb, va, vb, vc = refs
    scale = 1.0 / math.sqrt(DH)
    end = 0
    for ref in k_refs:
        at = slice(end, end + ref.shape[0])
        end += ref.shape[0]
        k1, k2, k3 = split3(ref[:, 0:DH])
        d1, d2 = split2(ref[:, DH : 2 * DH])
        v1, v2 = split2(ref[:, 2 * DH : 3 * DH])
        w1, w2 = split2(ref[:, 3 * DH : 4 * DH])
        ka[at, :] = jnp.concatenate([k1, k2, k1, k3, k1, k2], axis=1)
        kb[at, :] = jnp.concatenate([k1, d1, k2, d2, k1, d1], axis=1)
        va[at, :] = jnp.concatenate([v1, w1], axis=1)
        vb[at, :] = jnp.concatenate([v2, w2], axis=1)
        vc[at, :] = jnp.concatenate([v1, v2], axis=1)
    lane = lax.broadcasted_iota(jnp.int32, (rows, DH), 1)
    for b, ref in enumerate(q_refs):
        q = ref[:, 0:DH]
        a1, a2, a3 = split3(q * (scale * LOG2E))
        q1, q2 = split2(q * scale)
        d1, d2 = split2(ref[:, DH : 2 * DH] * scale)
        s = dot_nt(jnp.concatenate([a1, a1, a2, a1, a3, a2], axis=1), ka[...])
        st = dot_nt(jnp.concatenate([d1, q1, d1, q1, d2, q2], axis=1), kb[...])
        peak = jnp.max(s, axis=1, keepdims=True)
        if has_prev:
            old = prev[2 * b + 1][:, 0:3]
            peak = jnp.maximum(peak, old[:, 0:1])
        e = jnp.exp2(s - peak)
        w = e * st
        total = jnp.sum(e, axis=1, keepdims=True)
        total_t = jnp.sum(w, axis=1, keepdims=True)
        e1, e2 = split2(e)
        w1, w2 = split2(w)
        both = dot_nn(e1, va[...]) + dot_nn(e1, vb[...]) + dot_nn(e2, va[...])
        first = dot_nn(w1, vc[...])
        numer = both[:, :DH]
        numer_t = both[:, DH:] + first[:, :DH] + first[:, DH:] + dot_nn(w2, vc[:, :DH])
        if has_prev:
            factor = jnp.exp2(old[:, 0:1] - peak)
            total += factor * old[:, 1:2]
            total_t += factor * old[:, 2:3]
            numer += factor * prev[2 * b][:, :DH]
            numer_t += factor * prev[2 * b][:, DH:]
        stats = jnp.where(lane == 0, peak, jnp.where(lane == 1, total, total_t))
        if last:
            half = rows // 2
            for i in range(2):
                at = slice(i * half, (i + 1) * half)
                outs[2 * b + i][0:half, :DH] = numer[at]
                outs[2 * b + i][0:half, DH:] = numer_t[at]
                flat = stats[at].T[0:STAT_ROWS, :]
                outs[2 * b + i][half:, :] = jnp.concatenate([flat, jnp.zeros_like(flat)], axis=1)
        else:
            outs[2 * b][:, :DH] = numer
            outs[2 * b][:, DH:] = numer_t
            outs[2 * b + 1][...] = stats


def attend(q_blocks, k_blocks, prev, last):
    n_q, n_k, rows = len(q_blocks), len(k_blocks), q_blocks[0].shape[0]
    assert rows == 2 * DH
    keys = sum(x.shape[0] for x in k_blocks)
    shape = [f32(rows // 2 + STAT_ROWS, 2 * DH)] * 2 if last else [f32(rows, 2 * DH), f32(rows, DH)]
    work = n_q * rows * keys
    outs = pl.pallas_call(
        functools.partial(attend_kernel, n_q, n_k, rows, bool(prev), last),
        out_shape=shape * n_q,
        scratch_shapes=[pltpu.VMEM((keys, w * DH), jnp.bfloat16) for w in (6, 6, 2, 2, 2)],
        compiler_params=params(8 + keys * 16 // 1024),
        cost_estimate=pl.CostEstimate(
            flops=work * 2 * 256 * 18, transcendentals=work, bytes_accessed=n_q * rows * 4096 + keys * 2048
        ),
    )(*q_blocks, *k_blocks, *(x for pair in prev for x in pair))
    return [tuple(outs[i : i + 2]) for i in range(0, 2 * n_q, 2)]


def finish_kernel(n_q, core_ref, *refs):
    part_refs = refs[: 2 * n_q]
    out, tan = refs[2 * n_q :]
    rows = out.shape[0]
    for group, head in ((part_refs[0::2], core_ref[0]), (part_refs[1::2], 1 - core_ref[0])):
        wides = [
            jnp.concatenate(
                [ref[rows:, :DH], jnp.zeros((DH - STAT_ROWS, DH), jnp.float32)], axis=0
            ).T
            for ref in group
        ]
        peaks = [wide[:, 0:1] for wide in wides]
        top = functools.reduce(jnp.maximum, peaks)
        total = total_t = numer = numer_t = 0.0
        for ref, wide, peak in zip(group, wides, peaks):
            factor = jnp.exp2(peak - top)
            total += factor * wide[:, 1:2]
            total_t += factor * wide[:, 2:3]
            numer += factor * ref[0:rows, :DH]
            numer_t += factor * ref[0:rows, DH:]
        attended = numer / total
        column = pl.multiple_of(head * DH, DH)
        out[:, pl.ds(column, DH)] = attended
        tan[:, pl.ds(column, DH)] = (numer_t - attended * total_t) / total


def bits_of(n_pb, n_kv):
    low = n_kv.bit_length() - 1
    far = [1 << i for i in range(low)]
    near = [1 << (low + i) for i in range(1, n_pb.bit_length() - 1)]
    one = far[0::2] + near[1::2]
    two = far[1::2] + near[0::2]
    return ((one, two), (two, one)) if len(one) == len(two) else ((one, one), (two, two))


def per_device(n_pb, n_kv, *arrays):
    rows, width = arrays[0].shape
    assert width == 2 * DH and n_pb & (n_pb - 1) == 0 and n_kv & (n_kv - 1) == 0
    q_bits, k_bits = bits_of(n_pb, n_kv)
    core = (lax.axis_index("pb") % 2).astype(jnp.int32).reshape(1)

    def swap(x, masks, cross=False):
        flip = n_kv if cross else 0
        return lax.ppermute(
            x, AXES, [(i, i ^ flip ^ masks[i // n_kv % 2]) for i in range(n_pb * n_kv)]
        )

    smem = pl.BlockSpec(memory_space=pltpu.SMEM)
    vmem = pl.BlockSpec(memory_space=pltpu.VMEM)
    arrays = [arrays[i] for i in (0, 3, 1, 4, 2, 5)]
    own_q, own_k, give, give_k = pl.pallas_call(
        pack_kernel,
        out_shape=[f32(rows, w * DH) for w in (2, 4, 6, 4)],
        in_specs=[smem] + [vmem] * 6,
        compiler_params=params(8),
    )(core, *arrays)
    far = (k_bits[0][0], k_bits[1][0])
    got = swap(give, (0, 0), True)
    late_k = [swap(own_k, far), swap(give_k, far[::-1], True)]
    mine_q, mine_k = pl.pallas_call(
        join_kernel,
        out_shape=[f32(2 * rows, 2 * DH), f32(2 * rows, 4 * DH)],
        compiler_params=params(8),
    )(own_q, own_k, got)

    q_blocks = [mine_q]
    for masks in zip(*q_bits):
        q_blocks += [swap(x, masks) for x in q_blocks]
    early_k, forwarded = [mine_k] + late_k, []
    for masks in list(zip(*k_bits))[1:]:
        forwarded += [swap(x, masks) for x in late_k + forwarded]
        early_k += [swap(x, masks) for x in early_k if x is not late_k[0] and x is not late_k[1]]
    n_q = len(q_blocks)
    early_q = [i for i in range(n_q) if i & 1 == 0 or i == 1]
    states = dict(zip(early_q, attend([q_blocks[i] for i in early_q], early_k, [], False)))
    parts = {}
    for i in range(n_q - 1, -1, -1):
        if i not in states:
            parts[i] = attend([q_blocks[i]], early_k + forwarded, [], True)[0]
    for group in ([1], [i for i in early_q if i != 1]):
        prev = [states[i] for i in group]
        parts.update(zip(group, attend([q_blocks[i] for i in group], forwarded, prev, True)))

    def mask(bits, index):
        return sum(bit for i, bit in enumerate(bits) if index >> i & 1)

    back = []
    for i in range(n_q):
        masks = (mask(q_bits[0], i), mask(q_bits[1], i))
        back += [swap(parts[i][0], masks) if i else parts[i][0], swap(parts[i][1], masks, True)]
    return tuple(
        pl.pallas_call(
            functools.partial(finish_kernel, n_q),
            out_shape=[f32(rows, width)] * 2,
            in_specs=[smem] + [vmem] * (2 * n_q),
            compiler_params=params(8),
        )(core, *back)
    )


def solution(mesh):
    spec = P(AXES, None)
    body = functools.partial(per_device, mesh.shape["pb"], mesh.shape["kv"])
    return jax.shard_map(body, mesh=mesh, in_specs=(spec,) * 6, out_specs=(spec,) * 2, check_vma=False)
```

```python
import functools
import math

import jax
import jax.numpy as jnp
from jax import lax
from jax.experimental import pallas as pl
from jax.experimental.pallas import tpu as pltpu
from jax.sharding import PartitionSpec as P

DH = 128
LOG2E = 1.4426950408889634
STAT_ROWS = 8
AXES = ("pb", "kv")


def params(mib):
    return pltpu.CompilerParams(vmem_limit_bytes=int(mib * 1024 * 1024))


def split2(x):
    high = x.astype(jnp.bfloat16)
    return high, (x - high.astype(jnp.float32)).astype(jnp.bfloat16)


def split3(x):
    high = x.astype(jnp.bfloat16)
    rest = x - high.astype(jnp.float32)
    mid = rest.astype(jnp.bfloat16)
    return high, mid, (rest - mid.astype(jnp.float32)).astype(jnp.bfloat16)


def dot_nt(left, right):
    return lax.dot_general(
        left, right, (((1,), (1,)), ((), ())), preferred_element_type=jnp.float32
    )


def dot_nn(left, right):
    return jnp.dot(left, right, preferred_element_type=jnp.float32)


def f32(*shape):
    return jax.ShapeDtypeStruct(shape, jnp.float32)


def pack_kernel(*refs):
    ins, owns, (give, sems) = refs[:6], refs[6:12], refs[12:]
    core = lax.axis_index("pb") % 2
    own = pl.multiple_of(core * DH, DH)
    other = pl.multiple_of((1 - core) * DH, DH)
    moves = []
    for i, ref in enumerate(ins):
        moves.append((ref.at[:, pl.ds(own, DH)], owns[i]))
        moves.append((ref.at[:, pl.ds(other, DH)], give.at[:, i * DH : (i + 1) * DH]))
    copies = [pltpu.make_async_copy(src, dst, sems.at[i]) for i, (src, dst) in enumerate(moves)]
    for copy in copies:
        copy.start()
    for copy in copies:
        copy.wait()


def join_kernel(*refs):
    *owns, got, out_q, out_k = refs
    rows = got.shape[0]
    for i, ref in enumerate(owns):
        out, at = (out_q, i) if i < 2 else (out_k, i - 2)
        out[0:rows, at * DH : (at + 1) * DH] = ref[...]
    out_q[rows:, :] = got[:, 0 : 2 * DH]
    out_k[rows:, :] = got[:, 2 * DH :]


def attend_kernel(n_q, n_k, rows, has_prev, last, n_after, *refs):
    refs = list(refs)

    def take(count):
        head, refs[:] = refs[:count], refs[count:]
        return head

    q_refs, k_refs = take(n_q), take(n_k)
    prev = take(2 * n_q) if has_prev else None
    take(n_after)
    outs = take(2 * n_q)
    ka, kb, va, vb, vc = refs
    scale = 1.0 / math.sqrt(DH)
    end = 0
    for ref in k_refs:
        at = slice(end, end + ref.shape[0])
        end += ref.shape[0]
        k1, k2, k3 = split3(ref[:, 0:DH])
        d1, d2 = split2(ref[:, DH : 2 * DH])
        v1, v2 = split2(ref[:, 2 * DH : 3 * DH])
        w1, w2 = split2(ref[:, 3 * DH : 4 * DH])
        ka[at, :] = jnp.concatenate([k1, k2, k1, k3, k1, k2], axis=1)
        kb[at, :] = jnp.concatenate([k1, d1, k2, d2, k1, d1], axis=1)
        va[at, :] = jnp.concatenate([v1, w1], axis=1)
        vb[at, :] = jnp.concatenate([v2, w2], axis=1)
        vc[at, :] = jnp.concatenate([v1, v2], axis=1)
    lane = lax.broadcasted_iota(jnp.int32, (rows, DH), 1)
    for b, ref in enumerate(q_refs):
        q = ref[:, 0:DH]
        a1, a2, a3 = split3(q * (scale * LOG2E))
        q1, q2 = split2(q * scale)
        d1, d2 = split2(ref[:, DH : 2 * DH] * scale)
        s = dot_nt(jnp.concatenate([a1, a1, a2, a1, a3, a2], axis=1), ka[...])
        st = dot_nt(jnp.concatenate([d1, q1, d1, q1, d2, q2], axis=1), kb[...])
        peak = jnp.max(s, axis=1, keepdims=True)
        if has_prev:
            old = prev[2 * b + 1][:, 0:3]
            peak = jnp.maximum(peak, old[:, 0:1])
        e = jnp.exp2(s - peak)
        w = e * st
        total = jnp.sum(e, axis=1, keepdims=True)
        total_t = jnp.sum(w, axis=1, keepdims=True)
        e1, e2 = split2(e)
        w1, w2 = split2(w)
        both = dot_nn(e1, va[...]) + dot_nn(e1, vb[...]) + dot_nn(e2, va[...])
        first = dot_nn(w1, vc[...])
        numer = both[:, :DH]
        numer_t = both[:, DH:] + first[:, :DH] + first[:, DH:] + dot_nn(w2, vc[:, :DH])
        if has_prev:
            factor = jnp.exp2(old[:, 0:1] - peak)
            total += factor * old[:, 1:2]
            total_t += factor * old[:, 2:3]
            numer += factor * prev[2 * b][:, :DH]
            numer_t += factor * prev[2 * b][:, DH:]
        stats = jnp.where(lane == 0, peak, jnp.where(lane == 1, total, total_t))
        if last:
            half = rows // 2
            for i in range(2):
                at = slice(i * half, (i + 1) * half)
                outs[2 * b + i][0:half, :DH] = numer[at]
                outs[2 * b + i][0:half, DH:] = numer_t[at]
                flat = stats[at].T[0:STAT_ROWS, :]
                outs[2 * b + i][half:, :] = jnp.concatenate([flat, jnp.zeros_like(flat)], axis=1)
        else:
            outs[2 * b][:, :DH] = numer
            outs[2 * b][:, DH:] = numer_t
            outs[2 * b + 1][...] = stats


def attend(q_blocks, k_blocks, prev, last, after=()):
    n_q, n_k, rows = len(q_blocks), len(k_blocks), q_blocks[0].shape[0]
    assert rows == 2 * DH
    keys = sum(x.shape[0] for x in k_blocks)
    shape = [f32(rows // 2 + STAT_ROWS, 2 * DH)] * 2 if last else [f32(rows, 2 * DH), f32(rows, DH)]
    work = n_q * rows * keys
    outs = pl.pallas_call(
        functools.partial(attend_kernel, n_q, n_k, rows, bool(prev), last, len(after)),
        out_shape=shape * n_q,
        scratch_shapes=[pltpu.VMEM((keys, w * DH), jnp.bfloat16) for w in (6, 6, 2, 2, 2)],
        compiler_params=params(8 + keys * 16 // 1024),
        cost_estimate=pl.CostEstimate(
            flops=work * 2 * 256 * 18, transcendentals=work, bytes_accessed=n_q * rows * 4096 + keys * 2048
        ),
    )(*q_blocks, *k_blocks, *(x for pair in prev for x in pair), *after)
    return [tuple(outs[i : i + 2]) for i in range(0, 2 * n_q, 2)]


def finish_kernel(n_q, core_ref, *refs):
    part_refs = refs[: 2 * n_q]
    out, tan = refs[2 * n_q :]
    rows = out.shape[0]
    for group, head in ((part_refs[0::2], core_ref[0]), (part_refs[1::2], 1 - core_ref[0])):
        wides = [
            jnp.concatenate(
                [ref[rows:, :DH], jnp.zeros((DH - STAT_ROWS, DH), jnp.float32)], axis=0
            ).T
            for ref in group
        ]
        peaks = [wide[:, 0:1] for wide in wides]
        top = functools.reduce(jnp.maximum, peaks)
        total = total_t = numer = numer_t = 0.0
        for ref, wide, peak in zip(group, wides, peaks):
            factor = jnp.exp2(peak - top)
            total += factor * wide[:, 1:2]
            total_t += factor * wide[:, 2:3]
            numer += factor * ref[0:rows, :DH]
            numer_t += factor * ref[0:rows, DH:]
        attended = numer / total
        column = pl.multiple_of(head * DH, DH)
        out[:, pl.ds(column, DH)] = attended
        tan[:, pl.ds(column, DH)] = (numer_t - attended * total_t) / total


def bits_of(n_pb, n_kv):
    low = n_kv.bit_length() - 1
    far = [1 << i for i in range(low)]
    near = [1 << (low + i) for i in range(1, n_pb.bit_length() - 1)]
    one = far[0::2] + near[1::2]
    two = far[1::2] + near[0::2]
    return ((one, two), (two, one)) if len(one) == len(two) else ((one, one), (two, two))


def per_device(n_pb, n_kv, *arrays):
    rows, width = arrays[0].shape
    assert width == 2 * DH and n_pb & (n_pb - 1) == 0 and n_kv & (n_kv - 1) == 0
    q_bits, k_bits = bits_of(n_pb, n_kv)
    core = (lax.axis_index("pb") % 2).astype(jnp.int32).reshape(1)

    def swap(x, masks, cross=False):
        flip = n_kv if cross else 0
        return lax.ppermute(
            x, AXES, [(i, i ^ flip ^ masks[i // n_kv % 2]) for i in range(n_pb * n_kv)]
        )

    smem = pl.BlockSpec(memory_space=pltpu.SMEM)
    vmem = pl.BlockSpec(memory_space=pltpu.VMEM)
    arrays = [arrays[i] for i in (0, 3, 1, 4, 2, 5)]
    *owns, give = pl.pallas_call(
        pack_kernel,
        out_shape=[f32(rows, w * DH) for w in (1, 1, 1, 1, 1, 1, 6)],
        in_specs=[pl.BlockSpec(memory_space=pl.ANY)] * 6,
        out_specs=[vmem] * 6 + [pl.BlockSpec(memory_space=pl.ANY)],
        scratch_shapes=[pltpu.SemaphoreType.DMA((12,))],
        compiler_params=params(53.5),
    )(*arrays)
    got = swap(give, (0, 0), True)
    mine_q, mine_k = pl.pallas_call(
        join_kernel,
        out_shape=[f32(2 * rows, 2 * DH), f32(2 * rows, 4 * DH)],
        compiler_params=params(8),
    )(*owns, got)

    q_blocks = [mine_q]
    for masks in zip(*q_bits):
        q_blocks += [swap(x, masks) for x in q_blocks]
    k_blocks = [mine_k]
    for masks in zip(*k_bits):
        k_blocks += [swap(x, masks) for x in k_blocks]
    early_k = k_blocks[:1] + k_blocks[1:2] + k_blocks[2::2]
    forwarded = k_blocks[3::2]
    n_q = len(q_blocks)
    early_q = [i for i in range(n_q) if i & 1 == 0 or i == 1]
    states = dict(zip(early_q, attend([q_blocks[i] for i in early_q], early_k, [], False)))
    parts = {}
    for i in range(n_q - 1, -1, -1):
        if i not in states:
            parts[i] = attend([q_blocks[i]], early_k + forwarded, [], True, [states[0][1]])[0]
    for group in ([1], [i for i in early_q if i != 1]):
        prev = [states[i] for i in group]
        parts.update(zip(group, attend([q_blocks[i] for i in group], forwarded, prev, True)))

    def mask(bits, index):
        return sum(bit for i, bit in enumerate(bits) if index >> i & 1)

    back = []
    for i in range(n_q):
        masks = (mask(q_bits[0], i), mask(q_bits[1], i))
        back += [swap(parts[i][0], masks) if i else parts[i][0], swap(parts[i][1], masks, True)]
    return tuple(
        pl.pallas_call(
            functools.partial(finish_kernel, n_q),
            out_shape=[f32(rows, width)] * 2,
            in_specs=[smem] + [vmem] * (2 * n_q),
            compiler_params=params(8),
        )(core, *back)
    )


def solution(mesh):
    spec = P(AXES, None)
    body = functools.partial(per_device, mesh.shape["pb"], mesh.shape["kv"])
    return jax.shard_map(body, mesh=mesh, in_specs=(spec,) * 6, out_specs=(spec,) * 2, check_vma=False)
```

```python
import functools
import math

import jax
import jax.numpy as jnp
from jax import lax
from jax.experimental import pallas as pl
from jax.experimental.pallas import tpu as pltpu
from jax.sharding import PartitionSpec as P

DH = 128
LOG2E = 1.4426950408889634
STAT_ROWS = 8
AXES = ("pb", "kv")


def params(mib):
    return pltpu.CompilerParams(vmem_limit_bytes=int(mib * 1024 * 1024))


def split2(x):
    high = x.astype(jnp.bfloat16)
    return high, (x - high.astype(jnp.float32)).astype(jnp.bfloat16)


def split3(x):
    high = x.astype(jnp.bfloat16)
    rest = x - high.astype(jnp.float32)
    mid = rest.astype(jnp.bfloat16)
    return high, mid, (rest - mid.astype(jnp.float32)).astype(jnp.bfloat16)


def dot_nt(left, right):
    return lax.dot_general(
        left, right, (((1,), (1,)), ((), ())), preferred_element_type=jnp.float32
    )


def dot_nn(left, right):
    return jnp.dot(left, right, preferred_element_type=jnp.float32)


def f32(*shape):
    return jax.ShapeDtypeStruct(shape, jnp.float32)


def pack_kernel(*refs):
    ins, owns, (give, held, sems) = refs[:6], refs[6:12], refs[12:]
    core = lax.axis_index("pb") % 2
    own = pl.multiple_of(core * DH, DH)
    other = pl.multiple_of((1 - core) * DH, DH)
    copies = [pltpu.make_async_copy(ref, held.at[i], sems.at[i]) for i, ref in enumerate(ins)]
    for copy in copies:
        copy.start()
    for i, copy in enumerate(copies):
        copy.wait()
        owns[i][...] = held[i, :, pl.ds(own, DH)]
        give[:, i * DH : (i + 1) * DH] = held[i, :, pl.ds(other, DH)]


def join_kernel(*refs):
    *owns, got, out_q, out_k, out_kv = refs
    rows = got.shape[0]
    for i, ref in enumerate(owns):
        both = (ref[...], got[:, i * DH : (i + 1) * DH])
        for j, x in enumerate(both):
            at = slice(j * rows, (j + 1) * rows)
            if i < 2:
                out_q[at, i * DH : (i + 1) * DH] = x
            else:
                out_kv[at, (i - 2) * DH : (i - 1) * DH] = x
            if i in (2, 3):
                out_k[at, (i - 2) * DH : (i - 1) * DH] = x


def later_kernel(x, after, out):
    out[...] = x[:, x.shape[1] - out.shape[1] :]


def later(x, columns, after):
    return pl.pallas_call(
        later_kernel, out_shape=f32(x.shape[0], columns), compiler_params=params(8)
    )(x, after)


def attend_kernel(n_q, n_k, rows, has_prev, last, *refs):
    refs = list(refs)

    def take(count):
        head, refs[:] = refs[:count], refs[count:]
        return head

    q_refs, k_refs = take(n_q), [take(count) for count in n_k]
    prev = take(2 * n_q) if has_prev else None
    outs = take(2 * n_q)
    ka, kb, va, vb, vc = refs
    scale = 1.0 / math.sqrt(DH)
    for b, block in enumerate(k_refs):
        at = slice(b * rows, (b + 1) * rows)
        k, d, v, w = [ref[:, i : i + DH] for ref in block for i in range(0, ref.shape[1], DH)]
        k1, k2, k3 = split3(k)
        d1, d2 = split2(d)
        v1, v2 = split2(v)
        w1, w2 = split2(w)
        ka[at, :] = jnp.concatenate([k1, k2, k1, k3, k1, k2], axis=1)
        kb[at, :] = jnp.concatenate([k1, d1, k2, d2, k1, d1], axis=1)
        va[at, :] = jnp.concatenate([v1, w1], axis=1)
        vb[at, :] = jnp.concatenate([v2, w2], axis=1)
        vc[at, :] = jnp.concatenate([v1, v2], axis=1)
    lane = lax.broadcasted_iota(jnp.int32, (rows, DH), 1)
    for b, ref in enumerate(q_refs):
        q = ref[:, 0:DH]
        a1, a2, a3 = split3(q * (scale * LOG2E))
        q1, q2 = split2(q * scale)
        d1, d2 = split2(ref[:, DH : 2 * DH] * scale)
        s = dot_nt(jnp.concatenate([a1, a1, a2, a1, a3, a2], axis=1), ka[...])
        st = dot_nt(jnp.concatenate([d1, q1, d1, q1, d2, q2], axis=1), kb[...])
        peak = jnp.max(s, axis=1, keepdims=True)
        if has_prev:
            old = prev[2 * b + 1][:, 0:3]
            peak = jnp.maximum(peak, old[:, 0:1])
        e = jnp.exp2(s - peak)
        w = e * st
        total = jnp.sum(e, axis=1, keepdims=True)
        total_t = jnp.sum(w, axis=1, keepdims=True)
        e1, e2 = split2(e)
        w1, w2 = split2(w)
        both = dot_nn(e1, va[...]) + dot_nn(e1, vb[...]) + dot_nn(e2, va[...])
        first = dot_nn(w1, vc[...])
        numer = both[:, :DH]
        numer_t = both[:, DH:] + first[:, :DH] + first[:, DH:] + dot_nn(w2, vc[:, :DH])
        if has_prev:
            factor = jnp.exp2(old[:, 0:1] - peak)
            total += factor * old[:, 1:2]
            total_t += factor * old[:, 2:3]
            numer += factor * prev[2 * b][:, :DH]
            numer_t += factor * prev[2 * b][:, DH:]
        stats = jnp.where(lane == 0, peak, jnp.where(lane == 1, total, total_t))
        if last:
            half = rows // 2
            for i in range(2):
                at = slice(i * half, (i + 1) * half)
                outs[2 * b + i][0:half, :DH] = numer[at]
                outs[2 * b + i][0:half, DH:] = numer_t[at]
                flat = stats[at].T[0:STAT_ROWS, :]
                outs[2 * b + i][half:, :] = jnp.concatenate([flat, jnp.zeros_like(flat)], axis=1)
        else:
            outs[2 * b][:, :DH] = numer
            outs[2 * b][:, DH:] = numer_t
            outs[2 * b + 1][...] = stats


def attend(q_blocks, k_blocks, prev, last):
    n_q, n_k, rows = len(q_blocks), [len(block) for block in k_blocks], q_blocks[0].shape[0]
    assert rows == 2 * DH
    keys = rows * len(k_blocks)
    shape = [f32(rows // 2 + STAT_ROWS, 2 * DH)] * 2 if last else [f32(rows, 2 * DH), f32(rows, DH)]
    work = n_q * rows * keys
    outs = pl.pallas_call(
        functools.partial(attend_kernel, n_q, n_k, rows, bool(prev), last),
        out_shape=shape * n_q,
        scratch_shapes=[pltpu.VMEM((keys, w * DH), jnp.bfloat16) for w in (6, 6, 2, 2, 2)],
        compiler_params=params(8 + keys * 16 // 1024),
        cost_estimate=pl.CostEstimate(
            flops=work * 2 * 256 * 18, transcendentals=work, bytes_accessed=n_q * rows * 4096 + keys * 2048
        ),
    )(*q_blocks, *(x for block in k_blocks for x in block), *(x for pair in prev for x in pair))
    return [tuple(outs[i : i + 2]) for i in range(0, 2 * n_q, 2)]


def finish_kernel(n_q, core_ref, *refs):
    part_refs = refs[: 2 * n_q]
    out, tan = refs[2 * n_q :]
    rows = out.shape[0]
    for group, head in ((part_refs[0::2], core_ref[0]), (part_refs[1::2], 1 - core_ref[0])):
        wides = [
            jnp.concatenate(
                [ref[rows:, :DH], jnp.zeros((DH - STAT_ROWS, DH), jnp.float32)], axis=0
            ).T
            for ref in group
        ]
        peaks = [wide[:, 0:1] for wide in wides]
        top = functools.reduce(jnp.maximum, peaks)
        total = total_t = numer = numer_t = 0.0
        for ref, wide, peak in zip(group, wides, peaks):
            factor = jnp.exp2(peak - top)
            total += factor * wide[:, 1:2]
            total_t += factor * wide[:, 2:3]
            numer += factor * ref[0:rows, :DH]
            numer_t += factor * ref[0:rows, DH:]
        attended = numer / total
        column = pl.multiple_of(head * DH, DH)
        out[:, pl.ds(column, DH)] = attended
        tan[:, pl.ds(column, DH)] = (numer_t - attended * total_t) / total


def bits_of(n_pb, n_kv):
    low = n_kv.bit_length() - 1
    far = [1 << i for i in range(low)]
    near = [1 << (low + i) for i in range(1, n_pb.bit_length() - 1)]
    one = far[0::2] + near[1::2]
    two = far[1::2] + near[0::2]
    return ((one, two), (two, one)) if len(one) == len(two) else ((one, one), (two, two))


def per_device(n_pb, n_kv, *arrays):
    rows, width = arrays[0].shape
    assert width == 2 * DH and n_pb & (n_pb - 1) == 0 and n_kv & (n_kv - 1) == 0
    q_bits, k_bits = bits_of(n_pb, n_kv)
    core = (lax.axis_index("pb") % 2).astype(jnp.int32).reshape(1)

    def swap(x, masks, cross=False):
        flip = n_kv if cross else 0
        return lax.ppermute(
            x, AXES, [(i, i ^ flip ^ masks[i // n_kv % 2]) for i in range(n_pb * n_kv)]
        )

    smem = pl.BlockSpec(memory_space=pltpu.SMEM)
    vmem = pl.BlockSpec(memory_space=pltpu.VMEM)
    arrays = [arrays[i] for i in (0, 3, 1, 4, 2, 5)]
    *owns, give = pl.pallas_call(
        pack_kernel,
        out_shape=[f32(rows, w * DH) for w in (1, 1, 1, 1, 1, 1, 6)],
        in_specs=[pl.BlockSpec(memory_space=pl.ANY)] * 6,
        out_specs=[vmem] * 7,
        scratch_shapes=[pltpu.VMEM((6, rows, width), jnp.float32), pltpu.SemaphoreType.DMA((6,))],
        compiler_params=params(53.5),
    )(*arrays)
    got = swap(give, (0, 0), True)
    mine_q, mine_k, mine_kv = pl.pallas_call(
        join_kernel,
        out_shape=[f32(2 * rows, w * DH) for w in (2, 2, 4)],
        compiler_params=params(8),
    )(*owns, got)

    q_blocks, near_k = [mine_q], [(mine_kv,)]
    for masks in zip(*q_bits):
        q_blocks += [swap(x, masks) for x in q_blocks]
    (far, *near) = zip(*k_bits)
    for masks in near:
        near_k += [tuple(swap(x, masks) for x in block) for block in near_k]
    far_k = swap(mine_k, far)
    far_v = swap(later(mine_kv, 2 * DH, far_k), far)
    n_q = len(q_blocks)
    groups = [list(range(1, n_q, 2)), list(range(0, n_q, 2))]
    states, parts = {}, {}
    states.update(zip(groups[1], attend([q_blocks[i] for i in groups[1]], near_k, [], False)))
    last_k = [(far_k, later(far_v, 2 * DH, states[0][1]))]
    for masks in near:
        last_k += [tuple(swap(x, masks) for x in block) for block in last_k]
    states.update(zip(groups[0], attend([q_blocks[i] for i in groups[0]], near_k, [], False)))
    states = attend(q_blocks, [(far_k, far_v)], [states[i] for i in range(n_q)], False)
    for group in groups:
        done = attend([q_blocks[i] for i in group], last_k[1:], [states[i] for i in group], True)
        parts.update(zip(group, done))

    def mask(bits, index):
        return sum(bit for i, bit in enumerate(bits) if index >> i & 1)

    back = []
    for i in range(n_q):
        masks = (mask(q_bits[0], i), mask(q_bits[1], i))
        back += [swap(parts[i][0], masks) if i else parts[i][0], swap(parts[i][1], masks, True)]
    return tuple(
        pl.pallas_call(
            functools.partial(finish_kernel, n_q),
            out_shape=[f32(rows, width)] * 2,
            in_specs=[smem] + [vmem] * (2 * n_q),
            compiler_params=params(8),
        )(core, *back)
    )


def solution(mesh):
    spec = P(AXES, None)
    body = functools.partial(per_device, mesh.shape["pb"], mesh.shape["kv"])
    return jax.shard_map(body, mesh=mesh, in_specs=(spec,) * 6, out_specs=(spec,) * 2, check_vma=False)
```

```python
import functools
import math

import jax
import jax.numpy as jnp
from jax import lax
from jax.experimental import pallas as pl
from jax.experimental.pallas import tpu as pltpu
from jax.sharding import PartitionSpec as P

DH = 128
LOG2E = 1.4426950408889634
STAT_ROWS = 8
AXES = ("pb", "kv")


def params(mib):
    return pltpu.CompilerParams(vmem_limit_bytes=int(mib * 1024 * 1024))


def split2(x):
    high = x.astype(jnp.bfloat16)
    return high, (x - high.astype(jnp.float32)).astype(jnp.bfloat16)


def split3(x):
    high = x.astype(jnp.bfloat16)
    rest = x - high.astype(jnp.float32)
    mid = rest.astype(jnp.bfloat16)
    return high, mid, (rest - mid.astype(jnp.float32)).astype(jnp.bfloat16)


def dot_nt(left, right):
    return lax.dot_general(
        left, right, (((1,), (1,)), ((), ())), preferred_element_type=jnp.float32
    )


def dot_nn(left, right):
    return jnp.dot(left, right, preferred_element_type=jnp.float32)


def f32(*shape):
    return jax.ShapeDtypeStruct(shape, jnp.float32)


def pack_kernel(*refs):
    ins, owns, (give, held, sems) = refs[:6], refs[6:12], refs[12:]
    core = lax.axis_index("pb") % 2
    own = pl.multiple_of(core * DH, DH)
    other = pl.multiple_of((1 - core) * DH, DH)
    copies = [pltpu.make_async_copy(ref, held.at[i], sems.at[i]) for i, ref in enumerate(ins)]
    for copy in copies:
        copy.start()
    for i, copy in enumerate(copies):
        copy.wait()
        owns[i][...] = held[i, :, pl.ds(own, DH)]
        give[:, i * DH : (i + 1) * DH] = held[i, :, pl.ds(other, DH)]


def join_kernel(*refs):
    *owns, got, out_q, out_k, out_kv = refs
    rows = got.shape[0]
    for i, ref in enumerate(owns):
        both = (ref[...], got[:, i * DH : (i + 1) * DH])
        for j, x in enumerate(both):
            at = slice(j * rows, (j + 1) * rows)
            if i < 2:
                out_q[at, i * DH : (i + 1) * DH] = x
            else:
                out_kv[at, (i - 2) * DH : (i - 1) * DH] = x
            if i in (2, 3):
                out_k[at, (i - 2) * DH : (i - 1) * DH] = x


def later_kernel(x, after, out):
    out[...] = x[:, x.shape[1] - out.shape[1] :]


def later(x, columns, after):
    return pl.pallas_call(
        later_kernel, out_shape=f32(x.shape[0], columns), compiler_params=params(8)
    )(x, after)


def attend_kernel(n_q, n_k, rows, has_prev, last, *refs):
    refs = list(refs)

    def take(count):
        head, refs[:] = refs[:count], refs[count:]
        return head

    q_refs, k_refs = take(n_q), [take(count) for count in n_k]
    prev = take(2 * n_q) if has_prev else None
    outs = take(2 * n_q)
    ka, kb, va, vb, vc = refs
    scale = 1.0 / math.sqrt(DH)
    for b, block in enumerate(k_refs):
        at = slice(b * rows, (b + 1) * rows)
        k, d, v, w = [ref[:, i : i + DH] for ref in block for i in range(0, ref.shape[1], DH)]
        k1, k2, k3 = split3(k)
        d1, d2 = split2(d)
        v1, v2 = split2(v)
        w1, w2 = split2(w)
        ka[at, :] = jnp.concatenate([k1, k2, k1, k3, k1, k2], axis=1)
        kb[at, :] = jnp.concatenate([k1, d1, k2, d2, k1, d1], axis=1)
        va[at, :] = jnp.concatenate([v1, w1], axis=1)
        vb[at, :] = jnp.concatenate([v2, w2], axis=1)
        vc[at, :] = jnp.concatenate([v1, v2], axis=1)
    lane = lax.broadcasted_iota(jnp.int32, (rows, DH), 1)
    for b, ref in enumerate(q_refs):
        q = ref[:, 0:DH]
        a1, a2, a3 = split3(q * (scale * LOG2E))
        q1, q2 = split2(q * scale)
        d1, d2 = split2(ref[:, DH : 2 * DH] * scale)
        s = dot_nt(jnp.concatenate([a1, a1, a2, a1, a3, a2], axis=1), ka[...])
        st = dot_nt(jnp.concatenate([d1, q1, d1, q1, d2, q2], axis=1), kb[...])
        peak = jnp.max(s, axis=1, keepdims=True)
        if has_prev:
            old = prev[2 * b + 1][:, 0:3]
            peak = jnp.maximum(peak, old[:, 0:1])
        e = jnp.exp2(s - peak)
        w = e * st
        total = jnp.sum(e, axis=1, keepdims=True)
        total_t = jnp.sum(w, axis=1, keepdims=True)
        e1, e2 = split2(e)
        w1, w2 = split2(w)
        both = dot_nn(e1, va[...]) + dot_nn(e1, vb[...]) + dot_nn(e2, va[...])
        first = dot_nn(w1, vc[...])
        numer = both[:, :DH]
        numer_t = both[:, DH:] + first[:, :DH] + first[:, DH:] + dot_nn(w2, vc[:, :DH])
        if has_prev:
            factor = jnp.exp2(old[:, 0:1] - peak)
            total += factor * old[:, 1:2]
            total_t += factor * old[:, 2:3]
            numer += factor * prev[2 * b][:, :DH]
            numer_t += factor * prev[2 * b][:, DH:]
        if last:
            half = rows // 2
            for i in range(2):
                at = slice(i * half, (i + 1) * half)
                store_part(outs[2 * b + i], *(x[at] for x in (peak, total, total_t, numer, numer_t)))
        else:
            outs[2 * b][:, :DH] = numer
            outs[2 * b][:, DH:] = numer_t
            outs[2 * b + 1][...] = jnp.where(lane == 0, peak, jnp.where(lane == 1, total, total_t))


def attend(q_blocks, k_blocks, prev, last):
    n_q, n_k, rows = len(q_blocks), [len(block) for block in k_blocks], q_blocks[0].shape[0]
    assert rows == 2 * DH
    keys = rows * len(k_blocks)
    shape = [f32(rows // 2 + STAT_ROWS, 2 * DH)] * 2 if last else [f32(rows, 2 * DH), f32(rows, DH)]
    work = n_q * rows * keys
    outs = pl.pallas_call(
        functools.partial(attend_kernel, n_q, n_k, rows, bool(prev), last),
        out_shape=shape * n_q,
        scratch_shapes=[pltpu.VMEM((keys, w * DH), jnp.bfloat16) for w in (6, 6, 2, 2, 2)],
        compiler_params=params(8 + keys * 16 // 1024),
        cost_estimate=pl.CostEstimate(
            flops=work * 2 * 256 * 18, transcendentals=work, bytes_accessed=n_q * rows * 4096 + keys * 2048
        ),
    )(*q_blocks, *(x for block in k_blocks for x in block), *(x for pair in prev for x in pair))
    return [tuple(outs[i : i + 2]) for i in range(0, 2 * n_q, 2)]


def merge(refs):
    rows = refs[0].shape[0] - STAT_ROWS
    wides = [
        jnp.concatenate(
            [ref[rows:, :DH], jnp.zeros((DH - STAT_ROWS, DH), jnp.float32)], axis=0
        ).T
        for ref in refs
    ]
    peaks = [wide[:, 0:1] for wide in wides]
    top = functools.reduce(jnp.maximum, peaks)
    total = total_t = numer = numer_t = 0.0
    for ref, wide, peak in zip(refs, wides, peaks):
        factor = jnp.exp2(peak - top)
        total += factor * wide[:, 1:2]
        total_t += factor * wide[:, 2:3]
        numer += factor * ref[0:rows, :DH]
        numer_t += factor * ref[0:rows, DH:]
    return top, total, total_t, numer, numer_t


def store_part(out, peak, total, total_t, numer, numer_t):
    rows = out.shape[0] - STAT_ROWS
    lane = lax.broadcasted_iota(jnp.int32, (rows, DH), 1)
    stats = jnp.where(lane == 0, peak, jnp.where(lane == 1, total, total_t))
    flat = stats.T[0:STAT_ROWS, :]
    out[0:rows, :DH] = numer
    out[0:rows, DH:] = numer_t
    out[rows:, :] = jnp.concatenate([flat, jnp.zeros_like(flat)], axis=1)


def merge_kernel(one, two, out):
    store_part(out, *merge([one, two]))


def finish_kernel(n_own, core_ref, *refs):
    *part_refs, out, tan = refs
    for group, head in ((part_refs[:n_own], core_ref[0]), (part_refs[n_own:], 1 - core_ref[0])):
        _, total, total_t, numer, numer_t = merge(group)
        attended = numer / total
        column = pl.multiple_of(head * DH, DH)
        out[:, pl.ds(column, DH)] = attended
        tan[:, pl.ds(column, DH)] = (numer_t - attended * total_t) / total


def bits_of(n_pb, n_kv):
    low = n_kv.bit_length() - 1
    far = [1 << i for i in range(low)]
    near = [1 << (low + i) for i in range(1, n_pb.bit_length() - 1)]
    one = far[0::2] + near[1::2]
    two = far[1::2] + near[0::2]
    return ((one, two), (two, one)) if len(one) == len(two) else ((one, one), (two, two))


def per_device(n_pb, n_kv, *arrays):
    rows, width = arrays[0].shape
    assert width == 2 * DH and n_pb & (n_pb - 1) == 0 and n_kv & (n_kv - 1) == 0
    q_bits, k_bits = bits_of(n_pb, n_kv)
    core = (lax.axis_index("pb") % 2).astype(jnp.int32).reshape(1)

    def swap(x, masks, cross=False):
        flip = n_kv if cross else 0
        return lax.ppermute(
            x, AXES, [(i, i ^ flip ^ masks[i // n_kv % 2]) for i in range(n_pb * n_kv)]
        )

    smem = pl.BlockSpec(memory_space=pltpu.SMEM)
    vmem = pl.BlockSpec(memory_space=pltpu.VMEM)
    arrays = [arrays[i] for i in (0, 3, 1, 4, 2, 5)]
    *owns, give = pl.pallas_call(
        pack_kernel,
        out_shape=[f32(rows, w * DH) for w in (1, 1, 1, 1, 1, 1, 6)],
        in_specs=[pl.BlockSpec(memory_space=pl.ANY)] * 6,
        out_specs=[vmem] * 7,
        scratch_shapes=[pltpu.VMEM((6, rows, width), jnp.float32), pltpu.SemaphoreType.DMA((6,))],
        compiler_params=params(53.5),
    )(*arrays)
    got = swap(give, (0, 0), True)
    mine_q, mine_k, mine_kv = pl.pallas_call(
        join_kernel,
        out_shape=[f32(2 * rows, w * DH) for w in (2, 2, 4)],
        compiler_params=params(8),
    )(*owns, got)

    q_blocks, near_k = [mine_q], [(mine_kv,)]
    for masks in zip(*q_bits):
        q_blocks += [swap(x, masks) for x in q_blocks]
    (far, *near) = zip(*k_bits)
    for masks in near:
        near_k += [tuple(swap(x, masks) for x in block) for block in near_k]
    far_k = swap(mine_k, far)
    far_v = swap(later(mine_kv, 2 * DH, near_k[-1][0]), far)
    n_q = len(q_blocks)
    top_bit = n_q // 2
    far_q, near_q = list(range(1, n_q, 2)), list(range(0, n_q, 2))
    states = dict(zip(near_q, attend([q_blocks[i] for i in near_q], near_k, [], False)))
    last_k = [(far_k, later(far_v, 2 * DH, states[0][1]))]
    for masks in near:
        last_k += [tuple(swap(x, masks) for x in block) for block in last_k]
    states.update(zip(far_q, attend([q_blocks[i] for i in far_q], near_k, [], False)))
    states = attend(q_blocks, [(far_k, far_v)], [states[i] for i in range(n_q)], False)
    parts = {}
    for group in (
        [i for i in far_q if i & top_bit], [i for i in far_q if not i & top_bit], near_q
    ):
        done = attend([q_blocks[i] for i in group], last_k[1:], [states[i] for i in group], True)
        parts.update(zip(group, done))

    def masks_of(index):
        return tuple(sum(bit for i, bit in enumerate(bits) if index >> i & 1) for bits in q_bits)

    own = [parts[0][0]] + [swap(parts[i][0], masks_of(i)) for i in range(1, n_q)]
    cross = [swap(parts[0][1], masks_of(0), True), swap(parts[top_bit][1], masks_of(top_bit), True)]
    for i in range(1, top_bit):
        beside = swap(parts[i | top_bit][1], masks_of(top_bit))
        merged = pl.pallas_call(
            merge_kernel, out_shape=f32(rows + STAT_ROWS, 2 * DH), compiler_params=params(8)
        )(parts[i][1], beside)
        cross.append(swap(merged, masks_of(i), True))
    return tuple(
        pl.pallas_call(
            functools.partial(finish_kernel, n_q),
            out_shape=[f32(rows, width)] * 2,
            in_specs=[smem] + [vmem] * (n_q + len(cross)),
            compiler_params=params(8),
        )(core, *own, *cross)
    )


def solution(mesh):
    spec = P(AXES, None)
    body = functools.partial(per_device, mesh.shape["pb"], mesh.shape["kv"])
    return jax.shard_map(body, mesh=mesh, in_specs=(spec,) * 6, out_specs=(spec,) * 2, check_vma=False)
```

```python
import functools
import math

import jax
import jax.numpy as jnp
from jax import lax
from jax.experimental import pallas as pl
from jax.experimental.pallas import tpu as pltpu
from jax.sharding import PartitionSpec as P

DH = 128
LOG2E = 1.4426950408889634
STAT_ROWS = 8
AXES = ("pb", "kv")


def params(mib):
    return pltpu.CompilerParams(vmem_limit_bytes=int(mib * 1024 * 1024))


def split2(x):
    high = x.astype(jnp.bfloat16)
    return high, (x - high.astype(jnp.float32)).astype(jnp.bfloat16)


def split3(x):
    high = x.astype(jnp.bfloat16)
    rest = x - high.astype(jnp.float32)
    mid = rest.astype(jnp.bfloat16)
    return high, mid, (rest - mid.astype(jnp.float32)).astype(jnp.bfloat16)


def dot_nt(left, right):
    return lax.dot_general(
        left, right, (((1,), (1,)), ((), ())), preferred_element_type=jnp.float32
    )


def dot_nn(left, right):
    return jnp.dot(left, right, preferred_element_type=jnp.float32)


def f32(*shape):
    return jax.ShapeDtypeStruct(shape, jnp.float32)


def pack_kernel(*refs):
    ins, owns, (give, held, sems) = refs[:6], refs[6:12], refs[12:]
    core = lax.axis_index("pb") % 2
    own = pl.multiple_of(core * DH, DH)
    other = pl.multiple_of((1 - core) * DH, DH)
    copies = [pltpu.make_async_copy(ref, held.at[i], sems.at[i]) for i, ref in enumerate(ins)]
    for copy in copies:
        copy.start()
    for i, copy in enumerate(copies):
        copy.wait()
        owns[i][...] = held[i, :, pl.ds(own, DH)]
        give[:, i * DH : (i + 1) * DH] = held[i, :, pl.ds(other, DH)]


def join_kernel(*refs):
    *owns, got, out_q, out_k, out_kv = refs
    rows = got.shape[0]
    for i, ref in enumerate(owns):
        both = (ref[...], got[:, i * DH : (i + 1) * DH])
        for j, x in enumerate(both):
            at = slice(j * rows, (j + 1) * rows)
            if i < 2:
                out_q[at, i * DH : (i + 1) * DH] = x
            else:
                out_kv[at, (i - 2) * DH : (i - 1) * DH] = x
            if i in (2, 3):
                out_k[at, (i - 2) * DH : (i - 1) * DH] = x


def later_kernel(x, after, out):
    out[...] = x[:, x.shape[1] - out.shape[1] :]


def later(x, columns, after):
    return pl.pallas_call(
        later_kernel, out_shape=f32(x.shape[0], columns), compiler_params=params(8)
    )(x, after)


def attend_kernel(n_q, n_k, rows, has_prev, last, *refs):
    refs = list(refs)

    def take(count):
        head, refs[:] = refs[:count], refs[count:]
        return head

    q_refs, k_refs = take(n_q), [take(count) for count in n_k]
    prev = take(2 * n_q) if has_prev else None
    outs = take(2 * n_q)
    ka, kb, va, vb, vc = refs
    scale = 1.0 / math.sqrt(DH)
    for b, block in enumerate(k_refs):
        at = slice(b * rows, (b + 1) * rows)
        k, d, v, w = [ref[:, i : i + DH] for ref in block for i in range(0, ref.shape[1], DH)]
        k1, k2, k3 = split3(k)
        d1, d2 = split2(d)
        v1, v2 = split2(v)
        w1, w2 = split2(w)
        ka[at, :] = jnp.concatenate([k1, k2, k1, k3, k1, k2], axis=1)
        kb[at, :] = jnp.concatenate([k1, d1, k2, d2, k1, d1], axis=1)
        va[at, :] = jnp.concatenate([v1, w1], axis=1)
        vb[at, :] = jnp.concatenate([v2, w2], axis=1)
        vc[at, :] = jnp.concatenate([v1, v2], axis=1)
    lane = lax.broadcasted_iota(jnp.int32, (rows, DH), 1)
    for b, ref in enumerate(q_refs):
        q = ref[:, 0:DH]
        a1, a2, a3 = split3(q * (scale * LOG2E))
        q1, q2 = split2(q * scale)
        d1, d2 = split2(ref[:, DH : 2 * DH] * scale)
        s = dot_nt(jnp.concatenate([a1, a1, a2, a1, a3, a2], axis=1), ka[...])
        st = dot_nt(jnp.concatenate([d1, q1, d1, q1, d2, q2], axis=1), kb[...])
        peak = jnp.max(s, axis=1, keepdims=True)
        if has_prev:
            old = prev[2 * b + 1][:, 0:3]
            peak = jnp.maximum(peak, old[:, 0:1])
        e = jnp.exp2(s - peak)
        w = e * st
        total = jnp.sum(e, axis=1, keepdims=True)
        total_t = jnp.sum(w, axis=1, keepdims=True)
        e1, e2 = split2(e)
        w1, w2 = split2(w)
        both = dot_nn(e1, va[...]) + dot_nn(e1, vb[...]) + dot_nn(e2, va[...])
        first = dot_nn(w1, vc[...])
        numer = both[:, :DH]
        numer_t = both[:, DH:] + first[:, :DH] + first[:, DH:] + dot_nn(w2, vc[:, :DH])
        if has_prev:
            factor = jnp.exp2(old[:, 0:1] - peak)
            total += factor * old[:, 1:2]
            total_t += factor * old[:, 2:3]
            numer += factor * prev[2 * b][:, :DH]
            numer_t += factor * prev[2 * b][:, DH:]
        if last:
            half = rows // 2
            for i in range(2):
                at = slice(i * half, (i + 1) * half)
                store_part(outs[2 * b + i], *(x[at] for x in (peak, total, total_t, numer, numer_t)))
        else:
            outs[2 * b][:, :DH] = numer
            outs[2 * b][:, DH:] = numer_t
            outs[2 * b + 1][...] = jnp.where(lane == 0, peak, jnp.where(lane == 1, total, total_t))


def attend(q_blocks, k_blocks, prev, last):
    n_q, n_k, rows = len(q_blocks), [len(block) for block in k_blocks], q_blocks[0].shape[0]
    assert rows == 2 * DH
    keys = rows * len(k_blocks)
    shape = [f32(rows // 2 + STAT_ROWS, 2 * DH)] * 2 if last else [f32(rows, 2 * DH), f32(rows, DH)]
    work = n_q * rows * keys
    outs = pl.pallas_call(
        functools.partial(attend_kernel, n_q, n_k, rows, bool(prev), last),
        out_shape=shape * n_q,
        scratch_shapes=[pltpu.VMEM((keys, w * DH), jnp.bfloat16) for w in (6, 6, 2, 2, 2)],
        compiler_params=params(8 + keys * 16 // 1024),
        cost_estimate=pl.CostEstimate(
            flops=work * 2 * 256 * 18, transcendentals=work, bytes_accessed=n_q * rows * 4096 + keys * 2048
        ),
    )(*q_blocks, *(x for block in k_blocks for x in block), *(x for pair in prev for x in pair))
    return [tuple(outs[i : i + 2]) for i in range(0, 2 * n_q, 2)]


def merge(refs):
    rows = refs[0].shape[0] - STAT_ROWS
    wides = [
        jnp.concatenate(
            [ref[rows:, :DH], jnp.zeros((DH - STAT_ROWS, DH), jnp.float32)], axis=0
        ).T
        for ref in refs
    ]
    peaks = [wide[:, 0:1] for wide in wides]
    top = functools.reduce(jnp.maximum, peaks)
    total = total_t = numer = numer_t = 0.0
    for ref, wide, peak in zip(refs, wides, peaks):
        factor = jnp.exp2(peak - top)
        total += factor * wide[:, 1:2]
        total_t += factor * wide[:, 2:3]
        numer += factor * ref[0:rows, :DH]
        numer_t += factor * ref[0:rows, DH:]
    return top, total, total_t, numer, numer_t


def store_part(out, peak, total, total_t, numer, numer_t):
    rows = out.shape[0] - STAT_ROWS
    lane = lax.broadcasted_iota(jnp.int32, (rows, DH), 1)
    stats = jnp.where(lane == 0, peak, jnp.where(lane == 1, total, total_t))
    flat = stats.T[0:STAT_ROWS, :]
    out[0:rows, :DH] = numer
    out[0:rows, DH:] = numer_t
    out[rows:, :] = jnp.concatenate([flat, jnp.zeros_like(flat)], axis=1)


def merge_kernel(one, two, out):
    store_part(out, *merge([one, two]))


def finish_kernel(n_own, core_ref, *refs):
    *part_refs, out, tan = refs
    for group, head in ((part_refs[:n_own], core_ref[0]), (part_refs[n_own:], 1 - core_ref[0])):
        _, total, total_t, numer, numer_t = merge(group)
        attended = numer / total
        column = pl.multiple_of(head * DH, DH)
        out[:, pl.ds(column, DH)] = attended
        tan[:, pl.ds(column, DH)] = (numer_t - attended * total_t) / total


def bits_of(n_pb, n_kv):
    low = n_kv.bit_length() - 1
    far = [1 << i for i in range(low)]
    near = [1 << (low + i) for i in range(1, n_pb.bit_length() - 1)]
    one = far[0::2] + near[1::2]
    two = far[1::2] + near[0::2]
    return ((one, two), (two, one)) if len(one) == len(two) else ((one, one), (two, two))


def per_device(n_pb, n_kv, *arrays):
    rows, width = arrays[0].shape
    assert width == 2 * DH and n_pb & (n_pb - 1) == 0 and n_kv & (n_kv - 1) == 0
    q_bits, k_bits = bits_of(n_pb, n_kv)
    core = (lax.axis_index("pb") % 2).astype(jnp.int32).reshape(1)

    def swap(x, masks, cross=False):
        flip = n_kv if cross else 0
        return lax.ppermute(
            x, AXES, [(i, i ^ flip ^ masks[i // n_kv % 2]) for i in range(n_pb * n_kv)]
        )

    smem = pl.BlockSpec(memory_space=pltpu.SMEM)
    vmem = pl.BlockSpec(memory_space=pltpu.VMEM)
    arrays = [arrays[i] for i in (0, 3, 1, 4, 2, 5)]
    *owns, give = pl.pallas_call(
        pack_kernel,
        out_shape=[f32(rows, w * DH) for w in (1, 1, 1, 1, 1, 1, 6)],
        in_specs=[pl.BlockSpec(memory_space=pl.ANY)] * 6,
        out_specs=[vmem] * 7,
        scratch_shapes=[pltpu.VMEM((6, rows, width), jnp.float32), pltpu.SemaphoreType.DMA((6,))],
        compiler_params=params(53.5),
    )(*arrays)
    got = swap(give, (0, 0), True)
    mine_q, mine_k, mine_kv = pl.pallas_call(
        join_kernel,
        out_shape=[f32(2 * rows, w * DH) for w in (2, 2, 4)],
        compiler_params=params(8),
    )(*owns, got)

    near_k = [(mine_kv,)]
    (far, *near) = zip(*k_bits)
    for masks in near:
        near_k += [tuple(swap(x, masks) for x in block) for block in near_k]
    far_k = swap(mine_k, far)
    mine_v = later(mine_kv, 2 * DH, near_k[-1][0])
    far_v = swap(mine_v, far)
    q_blocks = [mine_q]
    for masks in zip(*q_bits):
        sent = [later(x, 2 * DH, mine_v) if i == 1 else x for i, x in enumerate(q_blocks)]
        q_blocks += [swap(x, masks) for x in sent]
    n_q = len(q_blocks)
    top_bit = n_q // 2
    far_q, near_q = list(range(1, n_q, 2)), list(range(0, n_q, 2))
    states = dict(zip(near_q, attend([q_blocks[i] for i in near_q], near_k, [], False)))
    last_k = [(later(far_k, 2 * DH, mine_v), later(far_v, 2 * DH, states[0][1]))]
    for masks in near:
        last_k += [tuple(swap(x, masks) for x in block) for block in last_k]
    far_kv = [(far_k, far_v)]
    first = [1] + near_q
    states[1] = attend([q_blocks[1]], near_k, [], False)[0]
    states.update(zip(first, attend([q_blocks[i] for i in first], far_kv, [states[i] for i in first], False)))
    rest = far_q[1:]
    if rest:
        blocks = [later(q_blocks[i], 2 * DH, states[1][1]) for i in rest]
        states.update(zip(rest, attend(blocks, near_k + far_kv, [], False)))
    parts = attend(q_blocks, last_k[1:], [states[i] for i in range(n_q)], True)

    def masks_of(index):
        return tuple(sum(bit for i, bit in enumerate(bits) if index >> i & 1) for bits in q_bits)

    own = [parts[0][0]] + [swap(parts[i][0], masks_of(i)) for i in range(1, n_q)]
    cross, merged = [], parts[0][1]
    for i in range(1, top_bit):
        beside = swap(parts[i | top_bit][1], masks_of(top_bit))
        merged = pl.pallas_call(
            merge_kernel, out_shape=f32(rows + STAT_ROWS, 2 * DH), compiler_params=params(8)
        )(parts[i][1], beside)
        cross.append(swap(merged, masks_of(i), True))
    for i in (top_bit, 0):
        cross.append(swap(later(parts[i][1], 2 * DH, merged), masks_of(i), True))
    return tuple(
        pl.pallas_call(
            functools.partial(finish_kernel, n_q),
            out_shape=[f32(rows, width)] * 2,
            in_specs=[smem] + [vmem] * (n_q + len(cross)),
            compiler_params=params(8),
        )(core, *own, *cross)
    )


def solution(mesh):
    spec = P(AXES, None)
    body = functools.partial(per_device, mesh.shape["pb"], mesh.shape["kv"])
    return jax.shard_map(body, mesh=mesh, in_specs=(spec,) * 6, out_specs=(spec,) * 2, check_vma=False)
```

```python
import functools
import math

import jax
import jax.numpy as jnp
from jax import lax
from jax.experimental import pallas as pl
from jax.experimental.pallas import tpu as pltpu
from jax.sharding import PartitionSpec as P

DH = 128
LOG2E = 1.4426950408889634
STAT_ROWS = 8
AXES = ("pb", "kv")


def params(mib):
    return pltpu.CompilerParams(vmem_limit_bytes=int(mib * 1024 * 1024))


def split2(x):
    high = x.astype(jnp.bfloat16)
    return high, (x - high.astype(jnp.float32)).astype(jnp.bfloat16)


def split3(x):
    high = x.astype(jnp.bfloat16)
    rest = x - high.astype(jnp.float32)
    mid = rest.astype(jnp.bfloat16)
    return high, mid, (rest - mid.astype(jnp.float32)).astype(jnp.bfloat16)


def dot_nt(left, right):
    return lax.dot_general(
        left, right, (((1,), (1,)), ((), ())), preferred_element_type=jnp.float32
    )


def dot_nn(left, right):
    return jnp.dot(left, right, preferred_element_type=jnp.float32)


def f32(*shape):
    return jax.ShapeDtypeStruct(shape, jnp.float32)


def pack_kernel(*refs):
    ins, owns, (give, held, sems) = refs[:6], refs[6:12], refs[12:]
    core = lax.axis_index("pb") % 2
    own = pl.multiple_of(core * DH, DH)
    other = pl.multiple_of((1 - core) * DH, DH)
    copies = [pltpu.make_async_copy(ref, held.at[i], sems.at[i]) for i, ref in enumerate(ins)]
    for copy in copies:
        copy.start()
    for i, copy in enumerate(copies):
        copy.wait()
        owns[i][...] = held[i, :, pl.ds(own, DH)]
        give[:, i * DH : (i + 1) * DH] = held[i, :, pl.ds(other, DH)]


def join_kernel(*refs):
    *owns, got, out_q, out_k, out_kv = refs
    rows = got.shape[0]
    for i, ref in enumerate(owns):
        both = (ref[...], got[:, i * DH : (i + 1) * DH])
        for j, x in enumerate(both):
            at = slice(j * rows, (j + 1) * rows)
            if i < 2:
                out_q[at, i * DH : (i + 1) * DH] = x
            else:
                out_kv[at, (i - 2) * DH : (i - 1) * DH] = x
            if i in (2, 3):
                out_k[at, (i - 2) * DH : (i - 1) * DH] = x


def later_kernel(x, after, out):
    out[...] = x[:, x.shape[1] - out.shape[1] :]


def later(x, columns, after):
    return pl.pallas_call(
        later_kernel, out_shape=f32(x.shape[0], columns), compiler_params=params(8)
    )(x, after)


def same_kernel(*refs):
    for ref, out in zip(refs[: len(refs) // 2], refs[len(refs) // 2 :]):
        out[...] = ref[...]


def landed(arrays):
    return pl.pallas_call(
        same_kernel, out_shape=[f32(*x.shape) for x in arrays], compiler_params=params(8)
    )(*arrays)


def halves_kernel(x, after, one, two):
    one[...] = x[:, :DH]
    two[...] = x[:, DH:]


def halves(x, after):
    return pl.pallas_call(
        halves_kernel, out_shape=[f32(x.shape[0], DH)] * 2, compiler_params=params(8)
    )(x, after)


def attend_kernel(n_q, n_k, rows, has_prev, last, split, *refs):
    refs = list(refs)

    def take(count):
        head, refs[:] = refs[:count], refs[count:]
        return head

    q_refs, k_refs = take(n_q), [take(count) for count in n_k]
    prev = take(2 * n_q) if has_prev else None
    outs = parts_of(take((3 if split else 2) * n_q), ([1, 2] if split else [1, 1]) * n_q)
    ka, kb, va, vb, vc = refs
    scale = 1.0 / math.sqrt(DH)
    for b, block in enumerate(k_refs):
        at = slice(b * rows, (b + 1) * rows)
        k, d, v, w = [ref[:, i : i + DH] for ref in block for i in range(0, ref.shape[1], DH)]
        k1, k2, k3 = split3(k)
        d1, d2 = split2(d)
        v1, v2 = split2(v)
        w1, w2 = split2(w)
        ka[at, :] = jnp.concatenate([k1, k2, k1, k3, k1, k2], axis=1)
        kb[at, :] = jnp.concatenate([k1, d1, k2, d2, k1, d1], axis=1)
        va[at, :] = jnp.concatenate([v1, w1], axis=1)
        vb[at, :] = jnp.concatenate([v2, w2], axis=1)
        vc[at, :] = jnp.concatenate([v1, v2], axis=1)
    lane = lax.broadcasted_iota(jnp.int32, (rows, DH), 1)
    for b, ref in enumerate(q_refs):
        q = ref[:, 0:DH]
        a1, a2, a3 = split3(q * (scale * LOG2E))
        q1, q2 = split2(q * scale)
        d1, d2 = split2(ref[:, DH : 2 * DH] * scale)
        s = dot_nt(jnp.concatenate([a1, a1, a2, a1, a3, a2], axis=1), ka[...])
        st = dot_nt(jnp.concatenate([d1, q1, d1, q1, d2, q2], axis=1), kb[...])
        peak = jnp.max(s, axis=1, keepdims=True)
        if has_prev:
            old = prev[2 * b + 1][:, 0:3]
            peak = jnp.maximum(peak, old[:, 0:1])
        e = jnp.exp2(s - peak)
        w = e * st
        total = jnp.sum(e, axis=1, keepdims=True)
        total_t = jnp.sum(w, axis=1, keepdims=True)
        e1, e2 = split2(e)
        w1, w2 = split2(w)
        both = dot_nn(e1, va[...]) + dot_nn(e1, vb[...]) + dot_nn(e2, va[...])
        first = dot_nn(w1, vc[...])
        numer = both[:, :DH]
        numer_t = both[:, DH:] + first[:, :DH] + first[:, DH:] + dot_nn(w2, vc[:, :DH])
        if has_prev:
            factor = jnp.exp2(old[:, 0:1] - peak)
            total += factor * old[:, 1:2]
            total_t += factor * old[:, 2:3]
            numer += factor * prev[2 * b][:, :DH]
            numer_t += factor * prev[2 * b][:, DH:]
        if last:
            half = rows // 2
            for i in range(2):
                at = slice(i * half, (i + 1) * half)
                store_part(outs[2 * b + i], *(x[at] for x in (peak, total, total_t, numer, numer_t)))
        else:
            outs[2 * b][0][:, :DH] = numer
            outs[2 * b][0][:, DH:] = numer_t
            outs[2 * b + 1][0][...] = jnp.where(lane == 0, peak, jnp.where(lane == 1, total, total_t))


def attend(q_blocks, k_blocks, prev, last, split=False):
    n_q, n_k, rows = len(q_blocks), [len(block) for block in k_blocks], q_blocks[0].shape[0]
    assert rows == 2 * DH
    keys = rows * len(k_blocks)
    if last:
        shape = part_shapes(rows // 2, 1) + part_shapes(rows // 2, 2 if split else 1)
    else:
        shape = [f32(rows, 2 * DH), f32(rows, DH)]
    work = n_q * rows * keys
    outs = pl.pallas_call(
        functools.partial(attend_kernel, n_q, n_k, rows, bool(prev), last, split),
        out_shape=shape * n_q,
        scratch_shapes=[pltpu.VMEM((keys, w * DH), jnp.bfloat16) for w in (6, 6, 2, 2, 2)],
        compiler_params=params(8 + keys * 16 // 1024),
        cost_estimate=pl.CostEstimate(
            flops=work * 2 * 256 * 18, transcendentals=work, bytes_accessed=n_q * rows * 4096 + keys * 2048
        ),
    )(*q_blocks, *(x for block in k_blocks for x in block), *(x for pair in prev for x in pair))
    return [tuple(outs[i : i + len(shape)]) for i in range(0, len(outs), len(shape))]


def parts_of(refs, counts):
    refs = iter(refs)
    return [tuple(next(refs) for _ in range(count)) for count in counts]


def merge(parts):
    rows = parts[0][0].shape[0] - STAT_ROWS
    wides = [
        jnp.concatenate(
            [part[0][rows:, :DH], jnp.zeros((DH - STAT_ROWS, DH), jnp.float32)], axis=0
        ).T
        for part in parts
    ]
    peaks = [wide[:, 0:1] for wide in wides]
    top = functools.reduce(jnp.maximum, peaks)
    total = total_t = numer = numer_t = 0.0
    for part, wide, peak in zip(parts, wides, peaks):
        factor = jnp.exp2(peak - top)
        total += factor * wide[:, 1:2]
        total_t += factor * wide[:, 2:3]
        numer += factor * part[0][0:rows, :DH]
        numer_t += factor * (part[1][...] if len(part) == 2 else part[0][0:rows, DH:])
    return top, total, total_t, numer, numer_t


def store_part(part, peak, total, total_t, numer, numer_t):
    rows = part[0].shape[0] - STAT_ROWS
    lane = lax.broadcasted_iota(jnp.int32, (rows, DH), 1)
    stats = jnp.where(lane == 0, peak, jnp.where(lane == 1, total, total_t))
    flat = stats.T[0:STAT_ROWS, :]
    part[0][0:rows, :DH] = numer
    part[0][rows:, :DH] = flat
    if len(part) == 2:
        part[1][...] = numer_t
    else:
        part[0][0:rows, DH:] = numer_t
        part[0][rows:, DH:] = jnp.zeros_like(flat)


def part_shapes(rows, count):
    if count == 2:
        return [f32(rows + STAT_ROWS, DH), f32(rows, DH)]
    return [f32(rows + STAT_ROWS, 2 * DH)]


def merge_kernel(one, two, out):
    store_part((out,), *merge([(one,), (two,)]))


def finish_kernel(n_own, counts, core_ref, *refs):
    *part_refs, out, tan = refs
    parts = parts_of(part_refs, counts)
    for group, head in ((parts[:n_own], core_ref[0]), (parts[n_own:], 1 - core_ref[0])):
        _, total, total_t, numer, numer_t = merge(group)
        attended = numer / total
        column = pl.multiple_of(head * DH, DH)
        out[:, pl.ds(column, DH)] = attended
        tan[:, pl.ds(column, DH)] = (numer_t - attended * total_t) / total


def bits_of(n_pb, n_kv):
    low = n_kv.bit_length() - 1
    far = [1 << i for i in range(low)]
    near = [1 << (low + i) for i in range(1, n_pb.bit_length() - 1)]
    one = far[0::2] + near[1::2]
    two = far[1::2] + near[0::2]
    return ((one, two), (two, one)) if len(one) == len(two) else ((one, one), (two, two))


def per_device(n_pb, n_kv, *arrays):
    rows, width = arrays[0].shape
    assert width == 2 * DH and n_pb & (n_pb - 1) == 0 and n_kv & (n_kv - 1) == 0
    q_bits, k_bits = bits_of(n_pb, n_kv)
    core = (lax.axis_index("pb") % 2).astype(jnp.int32).reshape(1)

    def swap(x, masks, cross=False):
        flip = n_kv if cross else 0
        return lax.ppermute(
            x, AXES, [(i, i ^ flip ^ masks[i // n_kv % 2]) for i in range(n_pb * n_kv)]
        )

    smem = pl.BlockSpec(memory_space=pltpu.SMEM)
    vmem = pl.BlockSpec(memory_space=pltpu.VMEM)
    arrays = [arrays[i] for i in (0, 3, 1, 4, 2, 5)]
    *owns, give = pl.pallas_call(
        pack_kernel,
        out_shape=[f32(rows, w * DH) for w in (1, 1, 1, 1, 1, 1, 6)],
        in_specs=[pl.BlockSpec(memory_space=pl.ANY)] * 6,
        out_specs=[vmem] * 7,
        scratch_shapes=[pltpu.VMEM((6, rows, width), jnp.float32), pltpu.SemaphoreType.DMA((6,))],
        compiler_params=params(53.5),
    )(*arrays)
    got = swap(give, (0, 0), True)
    mine_q, mine_k, mine_kv = pl.pallas_call(
        join_kernel,
        out_shape=[f32(2 * rows, w * DH) for w in (2, 2, 4)],
        compiler_params=params(8),
    )(*owns, got)

    near_k = [(mine_kv,)]
    (far, *near) = zip(*k_bits)
    for masks in near:
        near_k += [tuple(swap(x, masks) for x in block) for block in near_k]
    far_k = swap(mine_k, far)
    mine_v = later(mine_kv, 2 * DH, near_k[-1][0])
    far_v = swap(mine_v, far)
    q_blocks = [mine_q]
    for masks in zip(*q_bits):
        sent = [later(x, 2 * DH, mine_v) if i == 1 else x for i, x in enumerate(q_blocks)]
        q_blocks += [swap(x, masks) for x in sent]
    n_q = len(q_blocks)
    top_bit = n_q // 2
    far_q, near_q = list(range(1, n_q, 2)), list(range(0, n_q, 2))
    states = dict(zip(near_q, attend([q_blocks[i] for i in near_q], near_k, [], False)))
    last_k = [(later(far_k, 2 * DH, mine_v), *halves(far_v, states[0][1]))]
    for masks in near:
        last_k += [tuple(swap(x, masks) for x in block) for block in last_k]
    far_kv = [(far_k, far_v)]
    first = [1] + near_q
    states[1] = attend([q_blocks[1]], near_k, [], False)[0]
    states.update(zip(first, attend([q_blocks[i] for i in first], far_kv, [states[i] for i in first], False)))
    rest = far_q[1:]
    if rest:
        blocks = [later(q_blocks[i], 2 * DH, states[1][1]) for i in rest]
        states.update(zip(rest, attend(blocks, near_k + far_kv, [], False)))
    aside = [i for i in far_q if i & top_bit]
    parts = {}
    for group, split in ((aside, False), ([i for i in range(n_q) if i not in aside], False)):
        if group:
            done = attend(
                [q_blocks[i] for i in group], last_k[1:], [states[i] for i in group], True, split
            )
            parts.update(zip(group, done))

    def masks_of(index):
        return tuple(sum(bit for i, bit in enumerate(bits) if index >> i & 1) for bits in q_bits)

    own = [parts[0][0]] + [swap(parts[i][0], masks_of(i)) for i in range(1, n_q)]
    cross = []
    for i in range(1, top_bit):
        beside = [swap(x, masks_of(top_bit)) for x in parts[i | top_bit][1:]]
        merged = pl.pallas_call(
            merge_kernel, out_shape=part_shapes(rows, 1), compiler_params=params(8)
        )(parts[i][1], *beside)
        cross.append([swap(x, masks_of(i), True) for x in merged])
    for i in (top_bit, 0):
        cross.append((swap(parts[i][1], masks_of(i), True),))
    got = iter(landed([own[i] for i in far_q] + [x for part in cross[:-2] for x in part]))
    own = [next(got) if i in far_q else x for i, x in enumerate(own)]
    cross = [[next(got) for _ in part] for part in cross[:-2]] + cross[-2:]
    counts = [1] * n_q + [len(part) for part in cross]
    return tuple(
        pl.pallas_call(
            functools.partial(finish_kernel, n_q, counts),
            out_shape=[f32(rows, width)] * 2,
            in_specs=[smem] + [vmem] * sum(counts),
            compiler_params=params(8),
        )(core, *own, *(x for part in cross for x in part))
    )


def solution(mesh):
    spec = P(AXES, None)
    body = functools.partial(per_device, mesh.shape["pb"], mesh.shape["kv"])
    return jax.shard_map(body, mesh=mesh, in_specs=(spec,) * 6, out_specs=(spec,) * 2, check_vma=False)
```

```python
import functools
import math

import jax
import jax.numpy as jnp
from jax import lax
from jax.experimental import pallas as pl
from jax.experimental.pallas import tpu as pltpu
from jax.sharding import PartitionSpec as P

DH = 128
LOG2E = 1.4426950408889634
STAT_ROWS = 8
AXES = ("pb", "kv")


def params(mib):
    return pltpu.CompilerParams(vmem_limit_bytes=int(mib * 1024 * 1024))


def split2(x):
    high = x.astype(jnp.bfloat16)
    return high, (x - high.astype(jnp.float32)).astype(jnp.bfloat16)


def split3(x):
    high = x.astype(jnp.bfloat16)
    rest = x - high.astype(jnp.float32)
    mid = rest.astype(jnp.bfloat16)
    return high, mid, (rest - mid.astype(jnp.float32)).astype(jnp.bfloat16)


def dot_nt(left, right):
    return lax.dot_general(
        left, right, (((1,), (1,)), ((), ())), preferred_element_type=jnp.float32
    )


def dot_nn(left, right):
    return jnp.dot(left, right, preferred_element_type=jnp.float32)


def f32(*shape):
    return jax.ShapeDtypeStruct(shape, jnp.float32)


def pack_kernel(*refs):
    ins, owns, (give, held, sems) = refs[:6], refs[6:12], refs[12:]
    core = lax.axis_index("pb") % 2
    own = pl.multiple_of(core * DH, DH)
    other = pl.multiple_of((1 - core) * DH, DH)
    copies = [pltpu.make_async_copy(ref, held.at[i], sems.at[i]) for i, ref in enumerate(ins)]
    for copy in copies:
        copy.start()
    for i, copy in enumerate(copies):
        copy.wait()
        owns[i][...] = held[i, :, pl.ds(own, DH)]
        give[:, i * DH : (i + 1) * DH] = held[i, :, pl.ds(other, DH)]


def join_kernel(*refs):
    *owns, got, out_q, out_k, out_kv = refs
    rows = got.shape[0]
    for i, ref in enumerate(owns):
        both = (ref[...], got[:, i * DH : (i + 1) * DH])
        for j, x in enumerate(both):
            at = slice(j * rows, (j + 1) * rows)
            if i < 2:
                out_q[at, i * DH : (i + 1) * DH] = x
            else:
                out_kv[at, (i - 2) * DH : (i - 1) * DH] = x
            if i in (2, 3):
                out_k[at, (i - 2) * DH : (i - 1) * DH] = x


def later_kernel(x, after, out):
    out[...] = x[:, x.shape[1] - out.shape[1] :]


def later(x, columns, after):
    return pl.pallas_call(
        later_kernel, out_shape=f32(x.shape[0], columns), compiler_params=params(8)
    )(x, after)


def same_kernel(*refs):
    for ref, out in zip(refs[: len(refs) // 2], refs[len(refs) // 2 :]):
        out[...] = ref[...]


def landed(arrays):
    return pl.pallas_call(
        same_kernel, out_shape=[f32(*x.shape) for x in arrays], compiler_params=params(8)
    )(*arrays)


def same_kernel(*refs):
    for ref, out in zip(refs[: len(refs) // 2], refs[len(refs) // 2 :]):
        out[...] = ref[...]


def landed(arrays):
    return pl.pallas_call(
        same_kernel, out_shape=[f32(*x.shape) for x in arrays], compiler_params=params(8)
    )(*arrays)


def halves_kernel(x, after, one, two):
    one[...] = x[:, :DH]
    two[...] = x[:, DH:]


def halves(x, after):
    return pl.pallas_call(
        halves_kernel, out_shape=[f32(x.shape[0], DH)] * 2, compiler_params=params(8)
    )(x, after)


def attend_kernel(n_q, n_k, rows, has_prev, last, split, *refs):
    refs = list(refs)

    def take(count):
        head, refs[:] = refs[:count], refs[count:]
        return head

    q_refs, k_refs = take(n_q), [take(count) for count in n_k]
    prev = take(2 * n_q) if has_prev else None
    outs = parts_of(take((3 if split else 2) * n_q), ([1, 2] if split else [1, 1]) * n_q)
    ka, kb, va, vb, vc = refs
    scale = 1.0 / math.sqrt(DH)
    for b, block in enumerate(k_refs):
        at = slice(b * rows, (b + 1) * rows)
        k, d, v, w = [ref[:, i : i + DH] for ref in block for i in range(0, ref.shape[1], DH)]
        k1, k2, k3 = split3(k)
        d1, d2 = split2(d)
        v1, v2 = split2(v)
        w1, w2 = split2(w)
        ka[at, :] = jnp.concatenate([k1, k2, k1, k3, k1, k2], axis=1)
        kb[at, :] = jnp.concatenate([k1, d1, k2, d2, k1, d1], axis=1)
        va[at, :] = jnp.concatenate([v1, w1], axis=1)
        vb[at, :] = jnp.concatenate([v2, w2], axis=1)
        vc[at, :] = jnp.concatenate([v1, v2], axis=1)
    lane = lax.broadcasted_iota(jnp.int32, (rows, DH), 1)
    for b, ref in enumerate(q_refs):
        q = ref[:, 0:DH]
        a1, a2, a3 = split3(q * (scale * LOG2E))
        q1, q2 = split2(q * scale)
        d1, d2 = split2(ref[:, DH : 2 * DH] * scale)
        s = dot_nt(jnp.concatenate([a1, a1, a2, a1, a3, a2], axis=1), ka[...])
        st = dot_nt(jnp.concatenate([d1, q1, d1, q1, d2, q2], axis=1), kb[...])
        peak = jnp.max(s, axis=1, keepdims=True)
        if has_prev:
            old = prev[2 * b + 1][:, 0:3]
            peak = jnp.maximum(peak, old[:, 0:1])
        e = jnp.exp2(s - peak)
        w = e * st
        total = jnp.sum(e, axis=1, keepdims=True)
        total_t = jnp.sum(w, axis=1, keepdims=True)
        e1, e2 = split2(e)
        w1, w2 = split2(w)
        both = dot_nn(e1, va[...]) + dot_nn(e1, vb[...]) + dot_nn(e2, va[...])
        first = dot_nn(w1, vc[...])
        numer = both[:, :DH]
        numer_t = both[:, DH:] + first[:, :DH] + first[:, DH:] + dot_nn(w2, vc[:, :DH])
        if has_prev:
            factor = jnp.exp2(old[:, 0:1] - peak)
            total += factor * old[:, 1:2]
            total_t += factor * old[:, 2:3]
            numer += factor * prev[2 * b][:, :DH]
            numer_t += factor * prev[2 * b][:, DH:]
        if last:
            half = rows // 2
            for i in range(2):
                at = slice(i * half, (i + 1) * half)
                store_part(outs[2 * b + i], *(x[at] for x in (peak, total, total_t, numer, numer_t)))
        else:
            outs[2 * b][0][:, :DH] = numer
            outs[2 * b][0][:, DH:] = numer_t
            outs[2 * b + 1][0][...] = jnp.where(lane == 0, peak, jnp.where(lane == 1, total, total_t))


def attend(q_blocks, k_blocks, prev, last, split=False):
    n_q, n_k, rows = len(q_blocks), [len(block) for block in k_blocks], q_blocks[0].shape[0]
    assert rows == 2 * DH
    keys = rows * len(k_blocks)
    if last:
        shape = part_shapes(rows // 2, 1) + part_shapes(rows // 2, 2 if split else 1)
    else:
        shape = [f32(rows, 2 * DH), f32(rows, DH)]
    work = n_q * rows * keys
    outs = pl.pallas_call(
        functools.partial(attend_kernel, n_q, n_k, rows, bool(prev), last, split),
        out_shape=shape * n_q,
        scratch_shapes=[pltpu.VMEM((keys, w * DH), jnp.bfloat16) for w in (6, 6, 2, 2, 2)],
        compiler_params=params(8 + keys * 16 // 1024),
        cost_estimate=pl.CostEstimate(
            flops=work * 2 * 256 * 18, transcendentals=work, bytes_accessed=n_q * rows * 4096 + keys * 2048
        ),
    )(*q_blocks, *(x for block in k_blocks for x in block), *(x for pair in prev for x in pair))
    return [tuple(outs[i : i + len(shape)]) for i in range(0, len(outs), len(shape))]


def parts_of(refs, counts):
    refs = iter(refs)
    return [tuple(next(refs) for _ in range(count)) for count in counts]


def merge(parts):
    rows = parts[0][0].shape[0] - STAT_ROWS
    wides = [
        jnp.concatenate(
            [part[0][rows:, :DH], jnp.zeros((DH - STAT_ROWS, DH), jnp.float32)], axis=0
        ).T
        for part in parts
    ]
    peaks = [wide[:, 0:1] for wide in wides]
    top = functools.reduce(jnp.maximum, peaks)
    total = total_t = numer = numer_t = 0.0
    for part, wide, peak in zip(parts, wides, peaks):
        factor = jnp.exp2(peak - top)
        total += factor * wide[:, 1:2]
        total_t += factor * wide[:, 2:3]
        numer += factor * part[0][0:rows, :DH]
        numer_t += factor * (part[1][...] if len(part) == 2 else part[0][0:rows, DH:])
    return top, total, total_t, numer, numer_t


def store_part(part, peak, total, total_t, numer, numer_t):
    rows = part[0].shape[0] - STAT_ROWS
    lane = lax.broadcasted_iota(jnp.int32, (rows, DH), 1)
    stats = jnp.where(lane == 0, peak, jnp.where(lane == 1, total, total_t))
    flat = stats.T[0:STAT_ROWS, :]
    part[0][0:rows, :DH] = numer
    part[0][rows:, :DH] = flat
    if len(part) == 2:
        part[1][...] = numer_t
    else:
        part[0][0:rows, DH:] = numer_t
        part[0][rows:, DH:] = jnp.zeros_like(flat)


def part_shapes(rows, count):
    if count == 2:
        return [f32(rows + STAT_ROWS, DH), f32(rows, DH)]
    return [f32(rows + STAT_ROWS, 2 * DH)]


def merge_kernel(one, two, out):
    store_part((out,), *merge([(one,), (two,)]))


def finish_kernel(n_own, counts, core_ref, *refs):
    *part_refs, out, tan = refs
    parts = parts_of(part_refs, counts)
    for group, head in ((parts[:n_own], core_ref[0]), (parts[n_own:], 1 - core_ref[0])):
        _, total, total_t, numer, numer_t = merge(group)
        attended = numer / total
        column = pl.multiple_of(head * DH, DH)
        out[:, pl.ds(column, DH)] = attended
        tan[:, pl.ds(column, DH)] = (numer_t - attended * total_t) / total


def bits_of(n_pb, n_kv):
    low = n_kv.bit_length() - 1
    far = [1 << i for i in range(low)]
    near = [1 << (low + i) for i in range(1, n_pb.bit_length() - 1)]
    one = far[0::2] + near[1::2]
    two = far[1::2] + near[0::2]
    return ((one, two), (two, one)) if len(one) == len(two) else ((one, one), (two, two))


def per_device(n_pb, n_kv, *arrays):
    rows, width = arrays[0].shape
    assert width == 2 * DH and n_pb & (n_pb - 1) == 0 and n_kv & (n_kv - 1) == 0
    q_bits, k_bits = bits_of(n_pb, n_kv)
    core = (lax.axis_index("pb") % 2).astype(jnp.int32).reshape(1)

    def swap(x, masks, cross=False):
        flip = n_kv if cross else 0
        return lax.ppermute(
            x, AXES, [(i, i ^ flip ^ masks[i // n_kv % 2]) for i in range(n_pb * n_kv)]
        )

    smem = pl.BlockSpec(memory_space=pltpu.SMEM)
    vmem = pl.BlockSpec(memory_space=pltpu.VMEM)
    arrays = [arrays[i] for i in (0, 3, 1, 4, 2, 5)]
    *owns, give = pl.pallas_call(
        pack_kernel,
        out_shape=[f32(rows, w * DH) for w in (1, 1, 1, 1, 1, 1, 6)],
        in_specs=[pl.BlockSpec(memory_space=pl.ANY)] * 6,
        out_specs=[vmem] * 7,
        scratch_shapes=[pltpu.VMEM((6, rows, width), jnp.float32), pltpu.SemaphoreType.DMA((6,))],
        compiler_params=params(53.5),
    )(*arrays)
    got = swap(give, (0, 0), True)
    mine_q, mine_k, mine_kv = pl.pallas_call(
        join_kernel,
        out_shape=[f32(2 * rows, w * DH) for w in (2, 2, 4)],
        compiler_params=params(8),
    )(*owns, got)

    near_k = [(mine_kv,)]
    (far, *near) = zip(*k_bits)
    for masks in near:
        near_k += [tuple(swap(x, masks) for x in block) for block in near_k]
    far_k = swap(mine_k, far)
    mine_v = later(mine_kv, 2 * DH, near_k[-1][0])
    far_v = swap(mine_v, far)
    q_blocks = [mine_q]
    for masks in zip(*q_bits):
        sent = [later(x, 2 * DH, mine_v) if i == 1 else x for i, x in enumerate(q_blocks)]
        q_blocks += [swap(x, masks) for x in sent]
    n_q = len(q_blocks)
    top_bit = n_q // 2
    far_q, near_q = list(range(1, n_q, 2)), list(range(0, n_q, 2))
    states = dict(zip(near_q, attend([q_blocks[i] for i in near_q], near_k, [], False)))
    last_k = [(later(far_k, 2 * DH, mine_v), later(far_v, 2 * DH, states[0][1]))]
    for masks in near:
        last_k += [tuple(swap(x, masks) for x in block) for block in last_k]
    far_kv = [(far_k, far_v)]
    first = [1] + near_q
    states[1] = attend([q_blocks[1]], near_k, [], False)[0]
    states.update(zip(first, attend([q_blocks[i] for i in first], far_kv, [states[i] for i in first], False)))
    rest = far_q[1:]
    if rest:
        blocks = [later(q_blocks[i], 2 * DH, states[1][1]) for i in rest]
        states.update(zip(rest, attend(blocks, near_k + far_kv, [], False)))
    aside = [i for i in far_q if i & top_bit]
    parts = {}
    for group, split in ((aside, False), ([i for i in range(n_q) if i not in aside], False)):
        if group:
            done = attend(
                [q_blocks[i] for i in group], last_k[1:], [states[i] for i in group], True, split
            )
            parts.update(zip(group, done))

    def masks_of(index):
        return tuple(sum(bit for i, bit in enumerate(bits) if index >> i & 1) for bits in q_bits)

    own = [parts[0][0]] + [swap(parts[i][0], masks_of(i)) for i in range(1, n_q)]
    cross = []
    for i in range(1, top_bit):
        beside = [swap(x, masks_of(top_bit)) for x in parts[i | top_bit][1:]]
        merged = pl.pallas_call(
            merge_kernel, out_shape=part_shapes(rows, 1), compiler_params=params(8)
        )(parts[i][1], *beside)
        cross.append([swap(x, masks_of(i), True) for x in merged])
    for i in (top_bit, 0):
        cross.append((swap(later(parts[i][1], 2 * DH, own[-1]), masks_of(i), True),))
    got = iter(landed([own[i] for i in far_q] + [x for part in cross[:-2] for x in part]))
    own = [next(got) if i in far_q else x for i, x in enumerate(own)]
    cross = [[next(got) for _ in part] for part in cross[:-2]] + cross[-2:]
    counts = [1] * n_q + [len(part) for part in cross]
    return tuple(
        pl.pallas_call(
            functools.partial(finish_kernel, n_q, counts),
            out_shape=[f32(rows, width)] * 2,
            in_specs=[smem] + [vmem] * sum(counts),
            compiler_params=params(8),
        )(core, *own, *(x for part in cross for x in part))
    )


def solution(mesh):
    spec = P(AXES, None)
    body = functools.partial(per_device, mesh.shape["pb"], mesh.shape["kv"])
    return jax.shard_map(body, mesh=mesh, in_specs=(spec,) * 6, out_specs=(spec,) * 2, check_vma=False)
```

```python
import functools
import math

import jax
import jax.numpy as jnp
from jax import lax
from jax.experimental import pallas as pl
from jax.experimental.pallas import tpu as pltpu
from jax.sharding import PartitionSpec as P

DH = 128
LOG2E = 1.4426950408889634
STAT_ROWS = 8
AXES = ("pb", "kv")


def params(mib):
    return pltpu.CompilerParams(vmem_limit_bytes=int(mib * 1024 * 1024))


def split2(x):
    high = x.astype(jnp.bfloat16)
    return high, (x - high.astype(jnp.float32)).astype(jnp.bfloat16)


def split3(x):
    high = x.astype(jnp.bfloat16)
    rest = x - high.astype(jnp.float32)
    mid = rest.astype(jnp.bfloat16)
    return high, mid, (rest - mid.astype(jnp.float32)).astype(jnp.bfloat16)


def dot_nt(left, right):
    return lax.dot_general(
        left, right, (((1,), (1,)), ((), ())), preferred_element_type=jnp.float32
    )


def dot_nn(left, right):
    return jnp.dot(left, right, preferred_element_type=jnp.float32)


def f32(*shape):
    return jax.ShapeDtypeStruct(shape, jnp.float32)


def pack_kernel(*refs):
    ins, owns, (give, held, sems) = refs[:6], refs[6:12], refs[12:]
    core = lax.axis_index("pb") % 2
    own = pl.multiple_of(core * DH, DH)
    other = pl.multiple_of((1 - core) * DH, DH)
    copies = [pltpu.make_async_copy(ref, held.at[i], sems.at[i]) for i, ref in enumerate(ins)]
    for copy in copies:
        copy.start()
    for i, copy in enumerate(copies):
        copy.wait()
        owns[i][...] = held[i, :, pl.ds(own, DH)]
        give[:, i * DH : (i + 1) * DH] = held[i, :, pl.ds(other, DH)]


def join_kernel(*refs):
    *owns, got, out_q, out_k, out_kv = refs
    rows = got.shape[0]
    for i, ref in enumerate(owns):
        both = (ref[...], got[:, i * DH : (i + 1) * DH])
        for j, x in enumerate(both):
            at = slice(j * rows, (j + 1) * rows)
            if i < 2:
                out_q[at, i * DH : (i + 1) * DH] = x
            else:
                out_kv[at, (i - 2) * DH : (i - 1) * DH] = x
            if i in (2, 3):
                out_k[at, (i - 2) * DH : (i - 1) * DH] = x


def later_kernel(x, after, out):
    out[...] = x[:, x.shape[1] - out.shape[1] :]


def later(x, columns, after):
    return pl.pallas_call(
        later_kernel, out_shape=f32(x.shape[0], columns), compiler_params=params(8)
    )(x, after)


def same_kernel(*refs):
    for ref, out in zip(refs[: len(refs) // 2], refs[len(refs) // 2 :]):
        out[...] = ref[...]


def landed(arrays):
    return pl.pallas_call(
        same_kernel, out_shape=[f32(*x.shape) for x in arrays], compiler_params=params(8)
    )(*arrays)


def same_kernel(*refs):
    for ref, out in zip(refs[: len(refs) // 2], refs[len(refs) // 2 :]):
        out[...] = ref[...]


def landed(arrays):
    return pl.pallas_call(
        same_kernel, out_shape=[f32(*x.shape) for x in arrays], compiler_params=params(8)
    )(*arrays)


def halves_kernel(x, after, one, two):
    one[...] = x[:, :DH]
    two[...] = x[:, DH:]


def halves(x, after):
    return pl.pallas_call(
        halves_kernel, out_shape=[f32(x.shape[0], DH)] * 2, compiler_params=params(8)
    )(x, after)


def attend_kernel(n_q, n_k, rows, has_prev, last, split, *refs):
    refs = list(refs)

    def take(count):
        head, refs[:] = refs[:count], refs[count:]
        return head

    q_refs, k_refs = take(n_q), [take(count) for count in n_k]
    prev = take(2 * n_q) if has_prev else None
    outs = parts_of(take((3 if split else 2) * n_q), ([1, 2] if split else [1, 1]) * n_q)
    ka, kb, va, vb, vc = refs
    scale = 1.0 / math.sqrt(DH)
    for b, block in enumerate(k_refs):
        at = slice(b * rows, (b + 1) * rows)
        k, d, v, w = [ref[:, i : i + DH] for ref in block for i in range(0, ref.shape[1], DH)]
        k1, k2, k3 = split3(k)
        d1, d2 = split2(d)
        v1, v2 = split2(v)
        w1, w2 = split2(w)
        ka[at, :] = jnp.concatenate([k1, k2, k1, k3, k1, k2], axis=1)
        kb[at, :] = jnp.concatenate([k1, d1, k2, d2, k1, d1], axis=1)
        va[at, :] = jnp.concatenate([v1, w1], axis=1)
        vb[at, :] = jnp.concatenate([v2, w2], axis=1)
        vc[at, :] = jnp.concatenate([v1, v2], axis=1)
    lane = lax.broadcasted_iota(jnp.int32, (rows, DH), 1)
    for b, ref in enumerate(q_refs):
        q = ref[:, 0:DH]
        a1, a2, a3 = split3(q * (scale * LOG2E))
        q1, q2 = split2(q * scale)
        d1, d2 = split2(ref[:, DH : 2 * DH] * scale)
        s = dot_nt(jnp.concatenate([a1, a1, a2, a1, a3, a2], axis=1), ka[...])
        st = dot_nt(jnp.concatenate([d1, q1, d1, q1, d2, q2], axis=1), kb[...])
        peak = jnp.max(s, axis=1, keepdims=True)
        if has_prev:
            old = prev[2 * b + 1][:, 0:3]
            peak = jnp.maximum(peak, old[:, 0:1])
        e = jnp.exp2(s - peak)
        w = e * st
        total = jnp.sum(e, axis=1, keepdims=True)
        total_t = jnp.sum(w, axis=1, keepdims=True)
        e1, e2 = split2(e)
        w1, w2 = split2(w)
        both = dot_nn(e1, va[...]) + dot_nn(e1, vb[...]) + dot_nn(e2, va[...])
        first = dot_nn(w1, vc[...])
        numer = both[:, :DH]
        numer_t = both[:, DH:] + first[:, :DH] + first[:, DH:] + dot_nn(w2, vc[:, :DH])
        if has_prev:
            factor = jnp.exp2(old[:, 0:1] - peak)
            total += factor * old[:, 1:2]
            total_t += factor * old[:, 2:3]
            numer += factor * prev[2 * b][:, :DH]
            numer_t += factor * prev[2 * b][:, DH:]
        if last:
            half = rows // 2
            for i in range(2):
                at = slice(i * half, (i + 1) * half)
                store_part(outs[2 * b + i], *(x[at] for x in (peak, total, total_t, numer, numer_t)))
        else:
            outs[2 * b][0][:, :DH] = numer
            outs[2 * b][0][:, DH:] = numer_t
            outs[2 * b + 1][0][...] = jnp.where(lane == 0, peak, jnp.where(lane == 1, total, total_t))


def attend(q_blocks, k_blocks, prev, last, split=False):
    n_q, n_k, rows = len(q_blocks), [len(block) for block in k_blocks], q_blocks[0].shape[0]
    assert rows == 2 * DH
    keys = rows * len(k_blocks)
    if last:
        shape = part_shapes(rows // 2, 1) + part_shapes(rows // 2, 2 if split else 1)
    else:
        shape = [f32(rows, 2 * DH), f32(rows, DH)]
    work = n_q * rows * keys
    outs = pl.pallas_call(
        functools.partial(attend_kernel, n_q, n_k, rows, bool(prev), last, split),
        out_shape=shape * n_q,
        scratch_shapes=[pltpu.VMEM((keys, w * DH), jnp.bfloat16) for w in (6, 6, 2, 2, 2)],
        compiler_params=params(8 + keys * 16 // 1024),
        cost_estimate=pl.CostEstimate(
            flops=work * 2 * 256 * 18, transcendentals=work, bytes_accessed=n_q * rows * 4096 + keys * 2048
        ),
    )(*q_blocks, *(x for block in k_blocks for x in block), *(x for pair in prev for x in pair))
    return [tuple(outs[i : i + len(shape)]) for i in range(0, len(outs), len(shape))]


def parts_of(refs, counts):
    refs = iter(refs)
    return [tuple(next(refs) for _ in range(count)) for count in counts]


def merge(parts):
    rows = parts[0][0].shape[0] - STAT_ROWS
    wides = [
        jnp.concatenate(
            [part[0][rows:, :DH], jnp.zeros((DH - STAT_ROWS, DH), jnp.float32)], axis=0
        ).T
        for part in parts
    ]
    peaks = [wide[:, 0:1] for wide in wides]
    top = functools.reduce(jnp.maximum, peaks)
    total = total_t = numer = numer_t = 0.0
    for part, wide, peak in zip(parts, wides, peaks):
        factor = jnp.exp2(peak - top)
        total += factor * wide[:, 1:2]
        total_t += factor * wide[:, 2:3]
        numer += factor * part[0][0:rows, :DH]
        numer_t += factor * (part[1][...] if len(part) == 2 else part[0][0:rows, DH:])
    return top, total, total_t, numer, numer_t


def store_part(part, peak, total, total_t, numer, numer_t):
    rows = part[0].shape[0] - STAT_ROWS
    lane = lax.broadcasted_iota(jnp.int32, (rows, DH), 1)
    stats = jnp.where(lane == 0, peak, jnp.where(lane == 1, total, total_t))
    flat = stats.T[0:STAT_ROWS, :]
    part[0][0:rows, :DH] = numer
    part[0][rows:, :DH] = flat
    if len(part) == 2:
        part[1][...] = numer_t
    else:
        part[0][0:rows, DH:] = numer_t
        part[0][rows:, DH:] = jnp.zeros_like(flat)


def part_shapes(rows, count):
    if count == 2:
        return [f32(rows + STAT_ROWS, DH), f32(rows, DH)]
    return [f32(rows + STAT_ROWS, 2 * DH)]


def merge_kernel(one, two, out):
    store_part((out,), *merge([(one,), (two,)]))


def finish_kernel(n_own, counts, core_ref, *refs):
    *part_refs, out, tan = refs
    parts = parts_of(part_refs, counts)
    for group, head in ((parts[:n_own], core_ref[0]), (parts[n_own:], 1 - core_ref[0])):
        _, total, total_t, numer, numer_t = merge(group)
        attended = numer / total
        column = pl.multiple_of(head * DH, DH)
        out[:, pl.ds(column, DH)] = attended
        tan[:, pl.ds(column, DH)] = (numer_t - attended * total_t) / total


def bits_of(n_pb, n_kv):
    low = n_kv.bit_length() - 1
    far = [1 << i for i in range(low)]
    near = [1 << (low + i) for i in range(1, n_pb.bit_length() - 1)]
    one = far[0::2] + near[1::2]
    two = far[1::2] + near[0::2]
    return ((one, two), (two, one)) if len(one) == len(two) else ((one, one), (two, two))


def per_device(n_pb, n_kv, *arrays):
    rows, width = arrays[0].shape
    assert width == 2 * DH and n_pb & (n_pb - 1) == 0 and n_kv & (n_kv - 1) == 0
    q_bits, k_bits = bits_of(n_pb, n_kv)
    core = (lax.axis_index("pb") % 2).astype(jnp.int32).reshape(1)

    def swap(x, masks, cross=False):
        flip = n_kv if cross else 0
        return lax.ppermute(
            x, AXES, [(i, i ^ flip ^ masks[i // n_kv % 2]) for i in range(n_pb * n_kv)]
        )

    smem = pl.BlockSpec(memory_space=pltpu.SMEM)
    vmem = pl.BlockSpec(memory_space=pltpu.VMEM)
    arrays = [arrays[i] for i in (0, 3, 1, 4, 2, 5)]
    *owns, give = pl.pallas_call(
        pack_kernel,
        out_shape=[f32(rows, w * DH) for w in (1, 1, 1, 1, 1, 1, 6)],
        in_specs=[pl.BlockSpec(memory_space=pl.ANY)] * 6,
        out_specs=[vmem] * 7,
        scratch_shapes=[pltpu.VMEM((6, rows, width), jnp.float32), pltpu.SemaphoreType.DMA((6,))],
        compiler_params=params(53.5),
    )(*arrays)
    got = swap(give, (0, 0), True)
    mine_q, mine_k, mine_kv = pl.pallas_call(
        join_kernel,
        out_shape=[f32(2 * rows, w * DH) for w in (2, 2, 4)],
        compiler_params=params(8),
    )(*owns, got)

    near_k = [(mine_kv,)]
    (far, *near) = zip(*k_bits)
    for masks in near:
        near_k += [tuple(swap(x, masks) for x in block) for block in near_k]
    far_k = swap(mine_k, far)
    mine_v = later(mine_kv, 2 * DH, near_k[-1][0])
    far_v = swap(mine_v, far)
    q_blocks = [mine_q]
    for masks in zip(*q_bits):
        sent = [later(x, 2 * DH, mine_v) if i == 1 else x for i, x in enumerate(q_blocks)]
        q_blocks += [swap(x, masks) for x in sent]
    n_q = len(q_blocks)
    top_bit = n_q // 2
    far_q, near_q = list(range(1, n_q, 2)), list(range(0, n_q, 2))
    states = dict(zip(near_q, attend([q_blocks[i] for i in near_q], near_k, [], False)))
    last_k = [(later(far_k, 2 * DH, mine_v), later(far_v, 2 * DH, states[0][1]))]
    for masks in near:
        last_k += [tuple(swap(x, masks) for x in block) for block in last_k]
    far_kv = [(far_k, far_v)]
    first = [1] + near_q
    states[1] = attend([q_blocks[1]], near_k, [], False)[0]
    states.update(zip(first, attend([q_blocks[i] for i in first], far_kv, [states[i] for i in first], False)))
    rest = far_q[1:]
    if rest:
        blocks = [later(q_blocks[i], 2 * DH, states[1][1]) for i in rest]
        states.update(zip(rest, attend(blocks, near_k + far_kv, [], False)))
    aside = [i for i in far_q if i & top_bit]
    parts = {}

    def last_stage(group, after=None):
        prev = [states[i] for i in group]
        if after is not None:
            prev[0] = (prev[0][0], later(prev[0][1], DH, after))
        done = attend([q_blocks[i] for i in group], last_k[1:], prev, True)
        parts.update(zip(group, done))

    last_stage([i for i in far_q if i & top_bit])
    last_stage([i for i in far_q if not i & top_bit])

    def masks_of(index):
        return tuple(sum(bit for i, bit in enumerate(bits) if index >> i & 1) for bits in q_bits)

    own = {i: swap(parts[i][0], masks_of(i)) for i in far_q}
    cross, merged = [], None
    for i in far_q:
        if not i & top_bit:
            beside = swap(parts[i | top_bit][1], masks_of(top_bit))
            merged = pl.pallas_call(
                merge_kernel, out_shape=f32(rows + STAT_ROWS, 2 * DH), compiler_params=params(8)
            )(parts[i][1], beside)
            cross.append((swap(merged, masks_of(i), True),))
    last_stage(near_q, merged)
    own.update({i: swap(parts[i][0], masks_of(i)) if i else parts[i][0] for i in near_q})
    for i in [i for i in near_q if i & top_bit] + [i for i in near_q if not i & top_bit]:
        cross.append((swap(parts[i][1], masks_of(i), True),))
    far_cross = cross[: -len(near_q)]
    got = iter(landed([own[i] for i in far_q] + [x for part in far_cross for x in part]))
    own = [next(got) if i in far_q else own[i] for i in range(n_q)]
    cross = [(next(got),) for _ in far_cross] + cross[-len(near_q) :]
    counts = [1] * n_q + [len(part) for part in cross]
    return tuple(
        pl.pallas_call(
            functools.partial(finish_kernel, n_q, counts),
            out_shape=[f32(rows, width)] * 2,
            in_specs=[smem] + [vmem] * sum(counts),
            compiler_params=params(8),
        )(core, *own, *(x for part in cross for x in part))
    )


def solution(mesh):
    spec = P(AXES, None)
    body = functools.partial(per_device, mesh.shape["pb"], mesh.shape["kv"])
    return jax.shard_map(body, mesh=mesh, in_specs=(spec,) * 6, out_specs=(spec,) * 2, check_vma=False)
```

```python
import functools
import math

import jax
import jax.numpy as jnp
from jax import lax
from jax.experimental import pallas as pl
from jax.experimental.pallas import tpu as pltpu
from jax.sharding import PartitionSpec as P

DH = 128
LOG2E = 1.4426950408889634
STAT_ROWS = 8
AXES = ("pb", "kv")


def params(mib):
    return pltpu.CompilerParams(vmem_limit_bytes=int(mib * 1024 * 1024))


def split2(x):
    high = x.astype(jnp.bfloat16)
    return high, (x - high.astype(jnp.float32)).astype(jnp.bfloat16)


def split3(x):
    high = x.astype(jnp.bfloat16)
    rest = x - high.astype(jnp.float32)
    mid = rest.astype(jnp.bfloat16)
    return high, mid, (rest - mid.astype(jnp.float32)).astype(jnp.bfloat16)


def dot_nt(left, right):
    return lax.dot_general(
        left, right, (((1,), (1,)), ((), ())), preferred_element_type=jnp.float32
    )


def dot_nn(left, right):
    return jnp.dot(left, right, preferred_element_type=jnp.float32)


def f32(*shape):
    return jax.ShapeDtypeStruct(shape, jnp.float32)


def pack_kernel(*refs):
    ins, owns, (give, held, sems) = refs[:6], refs[6:12], refs[12:]
    core = lax.axis_index("pb") % 2
    own = pl.multiple_of(core * DH, DH)
    other = pl.multiple_of((1 - core) * DH, DH)
    copies = [pltpu.make_async_copy(ref, held.at[i], sems.at[i]) for i, ref in enumerate(ins)]
    for copy in copies:
        copy.start()
    for i, copy in enumerate(copies):
        copy.wait()
        owns[i][...] = held[i, :, pl.ds(own, DH)]
        give[:, i * DH : (i + 1) * DH] = held[i, :, pl.ds(other, DH)]


def join_kernel(*refs):
    *owns, got, out_q, out_k, out_kv = refs
    rows = got.shape[0]
    for i, ref in enumerate(owns):
        both = (ref[...], got[:, i * DH : (i + 1) * DH])
        for j, x in enumerate(both):
            at = slice(j * rows, (j + 1) * rows)
            if i < 2:
                out_q[at, i * DH : (i + 1) * DH] = x
            else:
                out_kv[at, (i - 2) * DH : (i - 1) * DH] = x
            if i in (2, 3):
                out_k[at, (i - 2) * DH : (i - 1) * DH] = x


def later_kernel(start, x, after, out):
    out[...] = x[:, start : start + out.shape[1]]


def later(x, columns, after, start=0):
    return pl.pallas_call(
        functools.partial(later_kernel, start),
        out_shape=f32(x.shape[0], columns),
        compiler_params=params(8),
    )(x, after)


def same_kernel(*refs):
    for ref, out in zip(refs[: len(refs) // 2], refs[len(refs) // 2 :]):
        out[...] = ref[...]


def landed(arrays):
    return pl.pallas_call(
        same_kernel, out_shape=[f32(*x.shape) for x in arrays], compiler_params=params(8)
    )(*arrays)


def attend_kernel(n_q, n_k, rows, has_prev, last, split, *refs):
    refs = list(refs)

    def take(count):
        head, refs[:] = refs[:count], refs[count:]
        return head

    q_refs, k_refs = take(n_q), [take(count) for count in n_k]
    prev = take(2 * n_q) if has_prev else None
    outs = parts_of(take((3 if split else 2) * n_q), ([1, 2] if split else [1, 1]) * n_q)
    ka, kb, va, vb, vc = refs
    scale = 1.0 / math.sqrt(DH)
    for b, block in enumerate(k_refs):
        at = slice(b * rows, (b + 1) * rows)
        k, d, v, w = [ref[:, i : i + DH] for ref in block for i in range(0, ref.shape[1], DH)]
        k1, k2, k3 = split3(k)
        d1, d2 = split2(d)
        v1, v2 = split2(v)
        w1, w2 = split2(w)
        ka[at, :] = jnp.concatenate([k1, k2, k1, k3, k1, k2], axis=1)
        kb[at, :] = jnp.concatenate([k1, d1, k2, d2, k1, d1], axis=1)
        va[at, :] = jnp.concatenate([v1, w1], axis=1)
        vb[at, :] = jnp.concatenate([v2, w2], axis=1)
        vc[at, :] = jnp.concatenate([v1, v2], axis=1)
    lane = lax.broadcasted_iota(jnp.int32, (rows, DH), 1)
    for b, ref in enumerate(q_refs):
        q = ref[:, 0:DH]
        a1, a2, a3 = split3(q * (scale * LOG2E))
        q1, q2 = split2(q * scale)
        d1, d2 = split2(ref[:, DH : 2 * DH] * scale)
        s = dot_nt(jnp.concatenate([a1, a1, a2, a1, a3, a2], axis=1), ka[...])
        st = dot_nt(jnp.concatenate([d1, q1, d1, q1, d2, q2], axis=1), kb[...])
        peak = jnp.max(s, axis=1, keepdims=True)
        if has_prev:
            old = prev[2 * b + 1][:, 0:3]
            peak = jnp.maximum(peak, old[:, 0:1])
        e = jnp.exp2(s - peak)
        w = e * st
        total = jnp.sum(e, axis=1, keepdims=True)
        total_t = jnp.sum(w, axis=1, keepdims=True)
        e1, e2 = split2(e)
        w1, w2 = split2(w)
        both = dot_nn(e1, va[...]) + dot_nn(e1, vb[...]) + dot_nn(e2, va[...])
        first = dot_nn(w1, vc[...])
        numer = both[:, :DH]
        numer_t = both[:, DH:] + first[:, :DH] + first[:, DH:] + dot_nn(w2, vc[:, :DH])
        if has_prev:
            factor = jnp.exp2(old[:, 0:1] - peak)
            total += factor * old[:, 1:2]
            total_t += factor * old[:, 2:3]
            numer += factor * prev[2 * b][:, :DH]
            numer_t += factor * prev[2 * b][:, DH:]
        if last:
            half = rows // 2
            for i in range(2):
                at = slice(i * half, (i + 1) * half)
                store_part(outs[2 * b + i], *(x[at] for x in (peak, total, total_t, numer, numer_t)))
        else:
            outs[2 * b][0][:, :DH] = numer
            outs[2 * b][0][:, DH:] = numer_t
            outs[2 * b + 1][0][...] = jnp.where(lane == 0, peak, jnp.where(lane == 1, total, total_t))


def attend(q_blocks, k_blocks, prev, last, split=False):
    n_q, n_k, rows = len(q_blocks), [len(block) for block in k_blocks], q_blocks[0].shape[0]
    assert rows == 2 * DH
    keys = rows * len(k_blocks)
    if last:
        shape = part_shapes(rows // 2, 1) + part_shapes(rows // 2, 2 if split else 1)
    else:
        shape = [f32(rows, 2 * DH), f32(rows, DH)]
    work = n_q * rows * keys
    outs = pl.pallas_call(
        functools.partial(attend_kernel, n_q, n_k, rows, bool(prev), last, split),
        out_shape=shape * n_q,
        scratch_shapes=[pltpu.VMEM((keys, w * DH), jnp.bfloat16) for w in (6, 6, 2, 2, 2)],
        compiler_params=params(8 + keys * 16 // 1024),
        cost_estimate=pl.CostEstimate(
            flops=work * 2 * 256 * 18, transcendentals=work, bytes_accessed=n_q * rows * 4096 + keys * 2048
        ),
    )(*q_blocks, *(x for block in k_blocks for x in block), *(x for pair in prev for x in pair))
    return [tuple(outs[i : i + len(shape)]) for i in range(0, len(outs), len(shape))]


def parts_of(refs, counts):
    refs = iter(refs)
    return [tuple(next(refs) for _ in range(count)) for count in counts]


def merge(parts):
    rows = parts[0][0].shape[0] - STAT_ROWS
    wides = [
        jnp.concatenate(
            [part[0][rows:, :DH], jnp.zeros((DH - STAT_ROWS, DH), jnp.float32)], axis=0
        ).T
        for part in parts
    ]
    peaks = [wide[:, 0:1] for wide in wides]
    top = functools.reduce(jnp.maximum, peaks)
    total = total_t = numer = numer_t = 0.0
    for part, wide, peak in zip(parts, wides, peaks):
        factor = jnp.exp2(peak - top)
        total += factor * wide[:, 1:2]
        total_t += factor * wide[:, 2:3]
        numer += factor * part[0][0:rows, :DH]
        numer_t += factor * (part[1][...] if len(part) == 2 else part[0][0:rows, DH:])
    return top, total, total_t, numer, numer_t


def store_part(part, peak, total, total_t, numer, numer_t):
    rows = part[0].shape[0] - STAT_ROWS
    lane = lax.broadcasted_iota(jnp.int32, (rows, DH), 1)
    stats = jnp.where(lane == 0, peak, jnp.where(lane == 1, total, total_t))
    flat = stats.T[0:STAT_ROWS, :]
    part[0][0:rows, :DH] = numer
    part[0][rows:, :DH] = flat
    if len(part) == 2:
        part[1][...] = numer_t
    else:
        part[0][0:rows, DH:] = numer_t
        part[0][rows:, DH:] = jnp.zeros_like(flat)


def part_shapes(rows, count):
    if count == 2:
        return [f32(rows + STAT_ROWS, DH), f32(rows, DH)]
    return [f32(rows + STAT_ROWS, 2 * DH)]


def merge_kernel(one, two, out):
    store_part((out,), *merge([(one,), (two,)]))


def finish_kernel(n_own, counts, core_ref, *refs):
    *part_refs, out, tan = refs
    parts = parts_of(part_refs, counts)
    for group, head in ((parts[:n_own], core_ref[0]), (parts[n_own:], 1 - core_ref[0])):
        _, total, total_t, numer, numer_t = merge(group)
        attended = numer / total
        column = pl.multiple_of(head * DH, DH)
        out[:, pl.ds(column, DH)] = attended
        tan[:, pl.ds(column, DH)] = (numer_t - attended * total_t) / total


def bits_of(n_pb, n_kv):
    low = n_kv.bit_length() - 1
    far = [1 << i for i in range(low)]
    near = [1 << (low + i) for i in range(1, n_pb.bit_length() - 1)]
    one = far[0::2] + near[1::2]
    two = far[1::2] + near[0::2]
    return ((one, two), (two, one)) if len(one) == len(two) else ((one, one), (two, two))


def per_device(n_pb, n_kv, *arrays):
    rows, width = arrays[0].shape
    assert width == 2 * DH and n_pb & (n_pb - 1) == 0 and n_kv & (n_kv - 1) == 0
    q_bits, k_bits = bits_of(n_pb, n_kv)
    core = (lax.axis_index("pb") % 2).astype(jnp.int32).reshape(1)

    def swap(x, masks, cross=False):
        flip = n_kv if cross else 0
        return lax.ppermute(
            x, AXES, [(i, i ^ flip ^ masks[i // n_kv % 2]) for i in range(n_pb * n_kv)]
        )

    smem = pl.BlockSpec(memory_space=pltpu.SMEM)
    vmem = pl.BlockSpec(memory_space=pltpu.VMEM)
    arrays = [arrays[i] for i in (0, 3, 1, 4, 2, 5)]
    *owns, give = pl.pallas_call(
        pack_kernel,
        out_shape=[f32(rows, w * DH) for w in (1, 1, 1, 1, 1, 1, 6)],
        in_specs=[pl.BlockSpec(memory_space=pl.ANY)] * 6,
        out_specs=[vmem] * 7,
        scratch_shapes=[pltpu.VMEM((6, rows, width), jnp.float32), pltpu.SemaphoreType.DMA((6,))],
        compiler_params=params(53.5),
    )(*arrays)
    got = swap(give, (0, 0), True)
    mine_q, mine_k, mine_kv = pl.pallas_call(
        join_kernel,
        out_shape=[f32(2 * rows, w * DH) for w in (2, 2, 4)],
        compiler_params=params(8),
    )(*owns, got)

    near_k = [(mine_kv,)]
    (far, *near) = zip(*k_bits)
    for masks in near:
        near_k += [tuple(swap(x, masks) for x in block) for block in near_k]
    far_k = swap(mine_k, far)
    mine_v = later(mine_kv, DH, near_k[-1][0], 2 * DH)
    sent_k = later(far_k, 2 * DH, mine_v)
    far_v = (swap(mine_v, far), swap(later(mine_kv, DH, sent_k, 3 * DH), far))
    q_blocks = [mine_q]
    for masks in zip(*q_bits):
        sent = [later(x, 2 * DH, mine_v) if i == 1 else x for i, x in enumerate(q_blocks)]
        q_blocks += [swap(x, masks) for x in sent]
    n_q = len(q_blocks)
    top_bit = n_q // 2
    far_q, near_q = list(range(1, n_q, 2)), list(range(0, n_q, 2))
    states = dict(zip(near_q, attend([q_blocks[i] for i in near_q], near_k, [], False)))
    last_k = [(sent_k, *(later(x, DH, states[0][1]) for x in far_v))]
    for masks in near:
        last_k += [tuple(swap(x, masks) for x in block) for block in last_k]
    far_kv = [(far_k, *far_v)]
    first = [1] + near_q
    states[1] = attend([q_blocks[1]], near_k, [], False)[0]
    states.update(zip(first, attend([q_blocks[i] for i in first], far_kv, [states[i] for i in first], False)))
    rest = far_q[1:]
    if rest:
        blocks = [later(q_blocks[i], 2 * DH, states[1][1]) for i in rest]
        states.update(zip(rest, attend(blocks, near_k + far_kv, [], False)))
    aside = [i for i in far_q if i & top_bit]
    parts = {}
    for group, split in ((aside, False), ([i for i in range(n_q) if i not in aside], False)):
        if group:
            done = attend(
                [q_blocks[i] for i in group], last_k[1:], [states[i] for i in group], True, split
            )
            parts.update(zip(group, done))

    def masks_of(index):
        return tuple(sum(bit for i, bit in enumerate(bits) if index >> i & 1) for bits in q_bits)

    own = [parts[0][0]] + [swap(parts[i][0], masks_of(i)) for i in range(1, n_q)]
    cross = []
    for i in range(1, top_bit):
        beside = [swap(x, masks_of(top_bit)) for x in parts[i | top_bit][1:]]
        merged = pl.pallas_call(
            merge_kernel, out_shape=part_shapes(rows, 1), compiler_params=params(8)
        )(parts[i][1], *beside)
        cross.append([swap(x, masks_of(i), True) for x in merged])
    for i in (top_bit, 0):
        cross.append((swap(parts[i][1], masks_of(i), True),))
    got = iter(landed([own[i] for i in far_q] + [x for part in cross[:-2] for x in part]))
    own = [next(got) if i in far_q else x for i, x in enumerate(own)]
    cross = [[next(got) for _ in part] for part in cross[:-2]] + cross[-2:]
    counts = [1] * n_q + [len(part) for part in cross]
    return tuple(
        pl.pallas_call(
            functools.partial(finish_kernel, n_q, counts),
            out_shape=[f32(rows, width)] * 2,
            in_specs=[smem] + [vmem] * sum(counts),
            compiler_params=params(8),
        )(core, *own, *(x for part in cross for x in part))
    )


def solution(mesh):
    spec = P(AXES, None)
    body = functools.partial(per_device, mesh.shape["pb"], mesh.shape["kv"])
    return jax.shard_map(body, mesh=mesh, in_specs=(spec,) * 6, out_specs=(spec,) * 2, check_vma=False)
```

```python
import functools
import math

import jax
import jax.numpy as jnp
from jax import lax
from jax.experimental import pallas as pl
from jax.experimental.pallas import tpu as pltpu
from jax.sharding import PartitionSpec as P

DH = 128
LOG2E = 1.4426950408889634
STAT_ROWS = 8
AXES = ("pb", "kv")


def params(mib):
    return pltpu.CompilerParams(vmem_limit_bytes=int(mib * 1024 * 1024))


def split2(x):
    high = x.astype(jnp.bfloat16)
    return high, (x - high.astype(jnp.float32)).astype(jnp.bfloat16)


def split3(x):
    high = x.astype(jnp.bfloat16)
    rest = x - high.astype(jnp.float32)
    mid = rest.astype(jnp.bfloat16)
    return high, mid, (rest - mid.astype(jnp.float32)).astype(jnp.bfloat16)


def dot_nt(left, right):
    return lax.dot_general(
        left, right, (((1,), (1,)), ((), ())), preferred_element_type=jnp.float32
    )


def dot_nn(left, right):
    return jnp.dot(left, right, preferred_element_type=jnp.float32)


def f32(*shape):
    return jax.ShapeDtypeStruct(shape, jnp.float32)


def pack_kernel(*refs):
    ins, owns, (give, held, sems) = refs[:6], refs[6:12], refs[12:]
    core = lax.axis_index("pb") % 2
    own = pl.multiple_of(core * DH, DH)
    other = pl.multiple_of((1 - core) * DH, DH)
    copies = [pltpu.make_async_copy(ref, held.at[i], sems.at[i]) for i, ref in enumerate(ins)]
    for copy in copies:
        copy.start()
    for i, copy in enumerate(copies):
        copy.wait()
        owns[i][...] = held[i, :, pl.ds(own, DH)]
        give[:, i * DH : (i + 1) * DH] = held[i, :, pl.ds(other, DH)]


def join_kernel(*refs):
    *owns, got, out_q, out_k, out_kv = refs
    rows = got.shape[0]
    for i, ref in enumerate(owns):
        both = (ref[...], got[:, i * DH : (i + 1) * DH])
        for j, x in enumerate(both):
            at = slice(j * rows, (j + 1) * rows)
            if i < 2:
                out_q[at, i * DH : (i + 1) * DH] = x
            else:
                out_kv[at, (i - 2) * DH : (i - 1) * DH] = x
            if i in (2, 3):
                out_k[at, (i - 2) * DH : (i - 1) * DH] = x


def later_kernel(x, after, out):
    out[...] = x[:, x.shape[1] - out.shape[1] :]


def later(x, columns, after):
    return pl.pallas_call(
        later_kernel, out_shape=f32(x.shape[0], columns), compiler_params=params(8)
    )(x, after)


def same_kernel(*refs):
    for ref, out in zip(refs[: len(refs) // 2], refs[len(refs) // 2 :]):
        out[...] = ref[...]


def landed(arrays):
    return pl.pallas_call(
        same_kernel, out_shape=[f32(*x.shape) for x in arrays], compiler_params=params(8)
    )(*arrays)


def attend_kernel(n_q, n_k, rows, has_prev, last, split, *refs):
    refs = list(refs)

    def take(count):
        head, refs[:] = refs[:count], refs[count:]
        return head

    q_refs, k_refs = take(n_q), [take(count) for count in n_k]
    prev = take(2 * n_q) if has_prev else None
    outs = parts_of(take((3 if split else 2) * n_q), ([1, 2] if split else [1, 1]) * n_q)
    ka, kb, va, vb, vc = refs
    scale = 1.0 / math.sqrt(DH)
    for b, block in enumerate(k_refs):
        at = slice(b * rows, (b + 1) * rows)
        k, d, v, w = [ref[:, i : i + DH] for ref in block for i in range(0, ref.shape[1], DH)]
        k1, k2, k3 = split3(k)
        d1, d2 = split2(d)
        v1, v2 = split2(v)
        w1, w2 = split2(w)
        ka[at, :] = jnp.concatenate([k1, k2, k1, k3, k1, k2], axis=1)
        kb[at, :] = jnp.concatenate([k1, d1, k2, d2, k1, d1], axis=1)
        va[at, :] = jnp.concatenate([v1, w1], axis=1)
        vb[at, :] = jnp.concatenate([v2, w2], axis=1)
        vc[at, :] = jnp.concatenate([v1, v2], axis=1)
    lane = lax.broadcasted_iota(jnp.int32, (rows, DH), 1)
    for b, ref in enumerate(q_refs):
        q = ref[:, 0:DH]
        a1, a2, a3 = split3(q * (scale * LOG2E))
        q1, q2 = split2(q * scale)
        d1, d2 = split2(ref[:, DH : 2 * DH] * scale)
        s = dot_nt(jnp.concatenate([a1, a1, a2, a1, a3, a2], axis=1), ka[...])
        st = dot_nt(jnp.concatenate([d1, q1, d1, q1, d2, q2], axis=1), kb[...])
        peak = jnp.max(s, axis=1, keepdims=True)
        if has_prev:
            old = prev[2 * b + 1][:, 0:3]
            peak = jnp.maximum(peak, old[:, 0:1])
        e = jnp.exp2(s - peak)
        w = e * st
        total = jnp.sum(e, axis=1, keepdims=True)
        total_t = jnp.sum(w, axis=1, keepdims=True)
        e1, e2 = split2(e)
        w1, w2 = split2(w)
        both = dot_nn(e1, va[...]) + dot_nn(e1, vb[...]) + dot_nn(e2, va[...])
        first = dot_nn(w1, vc[...])
        numer = both[:, :DH]
        numer_t = both[:, DH:] + first[:, :DH] + first[:, DH:] + dot_nn(w2, vc[:, :DH])
        if has_prev:
            factor = jnp.exp2(old[:, 0:1] - peak)
            total += factor * old[:, 1:2]
            total_t += factor * old[:, 2:3]
            numer += factor * prev[2 * b][:, :DH]
            numer_t += factor * prev[2 * b][:, DH:]
        if last:
            half = rows // 2
            for i in range(2):
                at = slice(i * half, (i + 1) * half)
                store_part(outs[2 * b + i], *(x[at] for x in (peak, total, total_t, numer, numer_t)))
        else:
            outs[2 * b][0][:, :DH] = numer
            outs[2 * b][0][:, DH:] = numer_t
            outs[2 * b + 1][0][...] = jnp.where(lane == 0, peak, jnp.where(lane == 1, total, total_t))


def attend(q_blocks, k_blocks, prev, last, split=False):
    n_q, n_k, rows = len(q_blocks), [len(block) for block in k_blocks], q_blocks[0].shape[0]
    assert rows == 2 * DH
    keys = rows * len(k_blocks)
    if last:
        shape = part_shapes(rows // 2, 1) + part_shapes(rows // 2, 2 if split else 1)
    else:
        shape = [f32(rows, 2 * DH), f32(rows, DH)]
    work = n_q * rows * keys
    outs = pl.pallas_call(
        functools.partial(attend_kernel, n_q, n_k, rows, bool(prev), last, split),
        out_shape=shape * n_q,
        scratch_shapes=[pltpu.VMEM((keys, w * DH), jnp.bfloat16) for w in (6, 6, 2, 2, 2)],
        compiler_params=params(8 + keys * 16 // 1024),
        cost_estimate=pl.CostEstimate(
            flops=work * 2 * 256 * 18, transcendentals=work, bytes_accessed=n_q * rows * 4096 + keys * 2048
        ),
    )(*q_blocks, *(x for block in k_blocks for x in block), *(x for pair in prev for x in pair))
    return [tuple(outs[i : i + len(shape)]) for i in range(0, len(outs), len(shape))]


def parts_of(refs, counts):
    refs = iter(refs)
    return [tuple(next(refs) for _ in range(count)) for count in counts]


def merge(parts):
    rows = parts[0][0].shape[0] - STAT_ROWS
    wides = [
        jnp.concatenate(
            [part[0][rows:, :DH], jnp.zeros((DH - STAT_ROWS, DH), jnp.float32)], axis=0
        ).T
        for part in parts
    ]
    peaks = [wide[:, 0:1] for wide in wides]
    top = functools.reduce(jnp.maximum, peaks)
    total = total_t = numer = numer_t = 0.0
    for part, wide, peak in zip(parts, wides, peaks):
        factor = jnp.exp2(peak - top)
        total += factor * wide[:, 1:2]
        total_t += factor * wide[:, 2:3]
        numer += factor * part[0][0:rows, :DH]
        numer_t += factor * (part[1][...] if len(part) == 2 else part[0][0:rows, DH:])
    return top, total, total_t, numer, numer_t


def store_part(part, peak, total, total_t, numer, numer_t):
    rows = part[0].shape[0] - STAT_ROWS
    lane = lax.broadcasted_iota(jnp.int32, (rows, DH), 1)
    stats = jnp.where(lane == 0, peak, jnp.where(lane == 1, total, total_t))
    flat = stats.T[0:STAT_ROWS, :]
    part[0][0:rows, :DH] = numer
    part[0][rows:, :DH] = flat
    if len(part) == 2:
        part[1][...] = numer_t
    else:
        part[0][0:rows, DH:] = numer_t
        part[0][rows:, DH:] = jnp.zeros_like(flat)


def part_shapes(rows, count):
    if count == 2:
        return [f32(rows + STAT_ROWS, DH), f32(rows, DH)]
    return [f32(rows + STAT_ROWS, 2 * DH)]


def merge_kernel(one, two, out):
    store_part((out,), *merge([(one,), (two,)]))


def finish_kernel(n_own, counts, core_ref, *refs):
    *part_refs, out, tan = refs
    parts = parts_of(part_refs, counts)
    for group, head in ((parts[:n_own], core_ref[0]), (parts[n_own:], 1 - core_ref[0])):
        _, total, total_t, numer, numer_t = merge(group)
        attended = numer / total
        column = pl.multiple_of(head * DH, DH)
        out[:, pl.ds(column, DH)] = attended
        tan[:, pl.ds(column, DH)] = (numer_t - attended * total_t) / total


def bits_of(n_pb, n_kv):
    low = n_kv.bit_length() - 1
    far = [1 << i for i in range(low)]
    near = [1 << (low + i) for i in range(1, n_pb.bit_length() - 1)]
    one = far[0::2] + near[1::2]
    two = far[1::2] + near[0::2]
    return ((one, two), (two, one)) if len(one) == len(two) else ((one, one), (two, two))


def per_device(n_pb, n_kv, *arrays):
    rows, width = arrays[0].shape
    assert width == 2 * DH and n_pb & (n_pb - 1) == 0 and n_kv & (n_kv - 1) == 0
    q_bits, k_bits = bits_of(n_pb, n_kv)
    core = (lax.axis_index("pb") % 2).astype(jnp.int32).reshape(1)

    def swap(x, masks, cross=False):
        flip = n_kv if cross else 0
        return lax.ppermute(
            x, AXES, [(i, i ^ flip ^ masks[i // n_kv % 2]) for i in range(n_pb * n_kv)]
        )

    smem = pl.BlockSpec(memory_space=pltpu.SMEM)
    vmem = pl.BlockSpec(memory_space=pltpu.VMEM)
    arrays = [arrays[i] for i in (0, 3, 1, 4, 2, 5)]
    *owns, give = pl.pallas_call(
        pack_kernel,
        out_shape=[f32(rows, w * DH) for w in (1, 1, 1, 1, 1, 1, 6)],
        in_specs=[pl.BlockSpec(memory_space=pl.ANY)] * 6,
        out_specs=[vmem] * 7,
        scratch_shapes=[pltpu.VMEM((6, rows, width), jnp.float32), pltpu.SemaphoreType.DMA((6,))],
        compiler_params=params(53.5),
    )(*arrays)
    got = swap(give, (0, 0), True)
    mine_q, mine_k, mine_kv = pl.pallas_call(
        join_kernel,
        out_shape=[f32(2 * rows, w * DH) for w in (2, 2, 4)],
        compiler_params=params(8),
    )(*owns, got)

    near_k = [(mine_kv,)]
    (far, *near) = zip(*k_bits)
    for masks in near:
        near_k += [tuple(swap(x, masks) for x in block) for block in near_k]
    far_k = swap(mine_k, far)
    mine_v = later(mine_kv, 2 * DH, near_k[-1][0])
    far_v = swap(mine_v, far)
    q_blocks = [mine_q]
    for masks in zip(*q_bits):
        sent = [later(x, 2 * DH, mine_v) if i == 1 else x for i, x in enumerate(q_blocks)]
        q_blocks += [swap(x, masks) for x in sent]
    n_q = len(q_blocks)
    top_bit = n_q // 2
    far_q, near_q = list(range(1, n_q, 2)), list(range(0, n_q, 2))
    states = dict(zip(near_q, attend([q_blocks[i] for i in near_q], near_k, [], False)))
    last_k = [(later(far_k, 2 * DH, mine_v), later(far_v, 2 * DH, states[0][1]))]
    for masks in near:
        last_k += [tuple(swap(x, masks) for x in block) for block in last_k]
    far_kv = [(far_k, far_v)]
    first = [1] + near_q
    states[1] = attend([q_blocks[1]], near_k, [], False)[0]
    states.update(zip(first, attend([q_blocks[i] for i in first], far_kv, [states[i] for i in first], False)))
    rest = far_q[1:]
    if rest:
        blocks = [later(q_blocks[i], 2 * DH, states[1][1]) for i in rest]
        states.update(zip(rest, attend(blocks, near_k + far_kv, [], False)))
    aside = [i for i in far_q if i & top_bit]
    parts = {}
    for group, split in ((aside, False), ([i for i in range(n_q) if i not in aside], False)):
        if group:
            done = attend(
                [q_blocks[i] for i in group], last_k[1:], [states[i] for i in group], True, split
            )
            parts.update(zip(group, done))

    def masks_of(index):
        return tuple(sum(bit for i, bit in enumerate(bits) if index >> i & 1) for bits in q_bits)

    own = [parts[0][0]] + [swap(parts[i][0], masks_of(i)) for i in range(1, n_q)]
    cross = []
    for i in range(1, top_bit):
        beside = [swap(x, masks_of(top_bit)) for x in parts[i | top_bit][1:]]
        merged = pl.pallas_call(
            merge_kernel, out_shape=part_shapes(rows, 1), compiler_params=params(8)
        )(parts[i][1], *beside)
        cross.append([swap(x, masks_of(i), True) for x in merged])
    for i in (top_bit, 0):
        cross.append((swap(parts[i][1], masks_of(i), True),))
    got = iter(landed([own[i] for i in far_q] + [x for part in cross[:-2] for x in part]))
    own = [next(got) if i in far_q else x for i, x in enumerate(own)]
    cross = [[next(got) for _ in part] for part in cross[:-2]] + cross[-2:]
    counts = [1] * n_q + [len(part) for part in cross]
    return tuple(
        pl.pallas_call(
            functools.partial(finish_kernel, n_q, counts),
            out_shape=[f32(rows, width)] * 2,
            in_specs=[smem] + [vmem] * sum(counts),
            compiler_params=params(8),
        )(core, *own, *(x for part in cross for x in part))
    )


def solution(mesh):
    spec = P(AXES, None)
    body = functools.partial(per_device, mesh.shape["pb"], mesh.shape["kv"])
    return jax.shard_map(body, mesh=mesh, in_specs=(spec,) * 6, out_specs=(spec,) * 2, check_vma=False)
```

```python
import functools
import math

import jax
import jax.numpy as jnp
from jax import lax
from jax.experimental import pallas as pl
from jax.experimental.pallas import tpu as pltpu
from jax.sharding import PartitionSpec as P

DH = 128
LOG2E = 1.4426950408889634
STAT_ROWS = 8
AXES = ("pb", "kv")


def params(mib):
    return pltpu.CompilerParams(vmem_limit_bytes=int(mib * 1024 * 1024))


def split2(x):
    high = x.astype(jnp.bfloat16)
    return high, (x - high.astype(jnp.float32)).astype(jnp.bfloat16)


def split3(x):
    high = x.astype(jnp.bfloat16)
    rest = x - high.astype(jnp.float32)
    mid = rest.astype(jnp.bfloat16)
    return high, mid, (rest - mid.astype(jnp.float32)).astype(jnp.bfloat16)


def dot_nt(left, right):
    return lax.dot_general(
        left, right, (((1,), (1,)), ((), ())), preferred_element_type=jnp.float32
    )


def dot_nn(left, right):
    return jnp.dot(left, right, preferred_element_type=jnp.float32)


def f32(*shape):
    return jax.ShapeDtypeStruct(shape, jnp.float32)


def pack_kernel(*refs):
    ins, owns, (give, held, sems) = refs[:6], refs[6:12], refs[12:]
    core = lax.axis_index("pb") % 2
    own = pl.multiple_of(core * DH, DH)
    other = pl.multiple_of((1 - core) * DH, DH)
    copies = [pltpu.make_async_copy(ref, held.at[i], sems.at[i]) for i, ref in enumerate(ins)]
    for copy in copies:
        copy.start()
    for i, copy in enumerate(copies):
        copy.wait()
        owns[i][...] = held[i, :, pl.ds(own, DH)]
        give[:, i * DH : (i + 1) * DH] = held[i, :, pl.ds(other, DH)]


def join_kernel(*refs):
    *owns, got, out_q, out_k, out_kv = refs
    rows = got.shape[0]
    for i, ref in enumerate(owns):
        both = (ref[...], got[:, i * DH : (i + 1) * DH])
        for j, x in enumerate(both):
            at = slice(j * rows, (j + 1) * rows)
            if i < 2:
                out_q[at, i * DH : (i + 1) * DH] = x
            else:
                out_kv[at, (i - 2) * DH : (i - 1) * DH] = x
            if i in (2, 3):
                out_k[at, (i - 2) * DH : (i - 1) * DH] = x


def later_kernel(x, after, out):
    out[...] = x[:, x.shape[1] - out.shape[1] :]


def later(x, columns, after):
    return pl.pallas_call(
        later_kernel, out_shape=f32(x.shape[0], columns), compiler_params=params(8)
    )(x, after)


def same_kernel(*refs):
    for ref, out in zip(refs[: len(refs) // 2], refs[len(refs) // 2 :]):
        out[...] = ref[...]


def landed(arrays):
    return pl.pallas_call(
        same_kernel, out_shape=[f32(*x.shape) for x in arrays], compiler_params=params(8)
    )(*arrays)


def halves_kernel(x, after, one, two):
    one[...] = x[:, :DH]
    two[...] = x[:, DH:]


def halves(x, after):
    return pl.pallas_call(
        halves_kernel, out_shape=[f32(x.shape[0], DH)] * 2, compiler_params=params(8)
    )(x, after)


def attend_kernel(n_q, n_k, rows, has_prev, last, split, *refs):
    refs = list(refs)

    def take(count):
        head, refs[:] = refs[:count], refs[count:]
        return head

    q_refs, k_refs = take(n_q), [take(count) for count in n_k]
    prev = take(2 * n_q) if has_prev else None
    outs = parts_of(take((3 if split else 2) * n_q), ([1, 2] if split else [1, 1]) * n_q)
    ka, kb, va, vb, vc = refs
    scale = 1.0 / math.sqrt(DH)
    for b, block in enumerate(k_refs):
        at = slice(b * rows, (b + 1) * rows)
        k, d, v, w = [ref[:, i : i + DH] for ref in block for i in range(0, ref.shape[1], DH)]
        k1, k2, k3 = split3(k)
        d1, d2 = split2(d)
        v1, v2 = split2(v)
        w1, w2 = split2(w)
        ka[at, :] = jnp.concatenate([k1, k2, k1, k3, k1, k2], axis=1)
        kb[at, :] = jnp.concatenate([k1, d1, k2, d2, k1, d1], axis=1)
        va[at, :] = jnp.concatenate([v1, w1], axis=1)
        vb[at, :] = jnp.concatenate([v2, w2], axis=1)
        vc[at, :] = jnp.concatenate([v1, v2], axis=1)
    lane = lax.broadcasted_iota(jnp.int32, (rows, DH), 1)
    for b, ref in enumerate(q_refs):
        q = ref[:, 0:DH]
        a1, a2, a3 = split3(q * (scale * LOG2E))
        q1, q2 = split2(q * scale)
        d1, d2 = split2(ref[:, DH : 2 * DH] * scale)
        s = dot_nt(jnp.concatenate([a1, a1, a2, a1, a3, a2], axis=1), ka[...])
        st = dot_nt(jnp.concatenate([d1, q1, d1, q1, d2, q2], axis=1), kb[...])
        peak = jnp.max(s, axis=1, keepdims=True)
        if has_prev:
            old = prev[2 * b + 1][:, 0:3]
            peak = jnp.maximum(peak, old[:, 0:1])
        e = jnp.exp2(s - peak)
        w = e * st
        total = jnp.sum(e, axis=1, keepdims=True)
        total_t = jnp.sum(w, axis=1, keepdims=True)
        e1, e2 = split2(e)
        w1, w2 = split2(w)
        both = dot_nn(e1, va[...]) + dot_nn(e1, vb[...]) + dot_nn(e2, va[...])
        first = dot_nn(w1, vc[...])
        numer = both[:, :DH]
        numer_t = both[:, DH:] + first[:, :DH] + first[:, DH:] + dot_nn(w2, vc[:, :DH])
        if has_prev:
            factor = jnp.exp2(old[:, 0:1] - peak)
            total += factor * old[:, 1:2]
            total_t += factor * old[:, 2:3]
            numer += factor * prev[2 * b][:, :DH]
            numer_t += factor * prev[2 * b][:, DH:]
        if last:
            half = rows // 2
            for i in range(2):
                at = slice(i * half, (i + 1) * half)
                store_part(outs[2 * b + i], *(x[at] for x in (peak, total, total_t, numer, numer_t)))
        else:
            outs[2 * b][0][:, :DH] = numer
            outs[2 * b][0][:, DH:] = numer_t
            outs[2 * b + 1][0][...] = jnp.where(lane == 0, peak, jnp.where(lane == 1, total, total_t))


def attend(q_blocks, k_blocks, prev, last, split=False):
    n_q, n_k, rows = len(q_blocks), [len(block) for block in k_blocks], q_blocks[0].shape[0]
    assert rows == 2 * DH
    keys = rows * len(k_blocks)
    if last:
        shape = part_shapes(rows // 2, 1) + part_shapes(rows // 2, 2 if split else 1)
    else:
        shape = [f32(rows, 2 * DH), f32(rows, DH)]
    work = n_q * rows * keys
    outs = pl.pallas_call(
        functools.partial(attend_kernel, n_q, n_k, rows, bool(prev), last, split),
        out_shape=shape * n_q,
        scratch_shapes=[pltpu.VMEM((keys, w * DH), jnp.bfloat16) for w in (6, 6, 2, 2, 2)],
        compiler_params=params(8 + keys * 16 // 1024),
        cost_estimate=pl.CostEstimate(
            flops=work * 2 * 256 * 18, transcendentals=work, bytes_accessed=n_q * rows * 4096 + keys * 2048
        ),
    )(*q_blocks, *(x for block in k_blocks for x in block), *(x for pair in prev for x in pair))
    return [tuple(outs[i : i + len(shape)]) for i in range(0, len(outs), len(shape))]


def parts_of(refs, counts):
    refs = iter(refs)
    return [tuple(next(refs) for _ in range(count)) for count in counts]


def merge(parts):
    rows = parts[0][0].shape[0] - STAT_ROWS
    wides = [
        jnp.concatenate(
            [part[0][rows:, :DH], jnp.zeros((DH - STAT_ROWS, DH), jnp.float32)], axis=0
        ).T
        for part in parts
    ]
    peaks = [wide[:, 0:1] for wide in wides]
    top = functools.reduce(jnp.maximum, peaks)
    total = total_t = numer = numer_t = 0.0
    for part, wide, peak in zip(parts, wides, peaks):
        factor = jnp.exp2(peak - top)
        total += factor * wide[:, 1:2]
        total_t += factor * wide[:, 2:3]
        numer += factor * part[0][0:rows, :DH]
        numer_t += factor * (part[1][...] if len(part) == 2 else part[0][0:rows, DH:])
    return top, total, total_t, numer, numer_t


def store_part(part, peak, total, total_t, numer, numer_t):
    rows = part[0].shape[0] - STAT_ROWS
    lane = lax.broadcasted_iota(jnp.int32, (rows, DH), 1)
    stats = jnp.where(lane == 0, peak, jnp.where(lane == 1, total, total_t))
    flat = stats.T[0:STAT_ROWS, :]
    part[0][0:rows, :DH] = numer
    part[0][rows:, :DH] = flat
    if len(part) == 2:
        part[1][...] = numer_t
    else:
        part[0][0:rows, DH:] = numer_t
        part[0][rows:, DH:] = jnp.zeros_like(flat)


def part_shapes(rows, count):
    if count == 2:
        return [f32(rows + STAT_ROWS, DH), f32(rows, DH)]
    return [f32(rows + STAT_ROWS, 2 * DH)]


def merge_kernel(one, two, out):
    store_part((out,), *merge([(one,), (two,)]))


def finish_kernel(n_own, counts, core_ref, *refs):
    *part_refs, out, tan = refs
    parts = parts_of(part_refs, counts)
    for group, head in ((parts[:n_own], core_ref[0]), (parts[n_own:], 1 - core_ref[0])):
        _, total, total_t, numer, numer_t = merge(group)
        attended = numer / total
        column = pl.multiple_of(head * DH, DH)
        out[:, pl.ds(column, DH)] = attended
        tan[:, pl.ds(column, DH)] = (numer_t - attended * total_t) / total


def bits_of(n_pb, n_kv):
    low = n_kv.bit_length() - 1
    far = [1 << i for i in range(low)]
    near = [1 << (low + i) for i in range(1, n_pb.bit_length() - 1)]
    one = far[0::2] + near[0::2]
    two = far[1::2] + near[1::2]
    return ((one, two), (two, one)) if len(one) == len(two) else ((one, one), (two, two))


def per_device(n_pb, n_kv, *arrays):
    rows, width = arrays[0].shape
    assert width == 2 * DH and n_pb & (n_pb - 1) == 0 and n_kv & (n_kv - 1) == 0
    q_bits, k_bits = bits_of(n_pb, n_kv)
    core = (lax.axis_index("pb") % 2).astype(jnp.int32).reshape(1)

    def swap(x, masks, cross=False):
        flip = n_kv if cross else 0
        return lax.ppermute(
            x, AXES, [(i, i ^ flip ^ masks[i // n_kv % 2]) for i in range(n_pb * n_kv)]
        )

    smem = pl.BlockSpec(memory_space=pltpu.SMEM)
    vmem = pl.BlockSpec(memory_space=pltpu.VMEM)
    arrays = [arrays[i] for i in (0, 3, 1, 4, 2, 5)]
    *owns, give = pl.pallas_call(
        pack_kernel,
        out_shape=[f32(rows, w * DH) for w in (1, 1, 1, 1, 1, 1, 6)],
        in_specs=[pl.BlockSpec(memory_space=pl.ANY)] * 6,
        out_specs=[vmem] * 7,
        scratch_shapes=[pltpu.VMEM((6, rows, width), jnp.float32), pltpu.SemaphoreType.DMA((6,))],
        compiler_params=params(53.5),
    )(*arrays)
    got = swap(give, (0, 0), True)
    mine_q, mine_k, mine_kv = pl.pallas_call(
        join_kernel,
        out_shape=[f32(2 * rows, w * DH) for w in (2, 2, 4)],
        compiler_params=params(8),
    )(*owns, got)

    near_k = [(mine_kv,)]
    (far, *near) = zip(*k_bits)
    for masks in near:
        near_k += [tuple(swap(x, masks) for x in block) for block in near_k]
    far_k = swap(mine_k, far)
    mine_v = later(mine_kv, 2 * DH, near_k[-1][0])
    far_v = swap(mine_v, far)
    q_blocks = [mine_q]
    for masks in zip(*q_bits):
        sent = [later(x, 2 * DH, mine_v) if i == 1 else x for i, x in enumerate(q_blocks)]
        q_blocks += [swap(x, masks) for x in sent]
    n_q = len(q_blocks)
    top_bit = n_q // 2
    far_q, near_q = list(range(1, n_q, 2)), list(range(0, n_q, 2))
    states = dict(zip(near_q, attend([q_blocks[i] for i in near_q], near_k, [], False)))
    last_k = [(later(far_k, 2 * DH, mine_v), *halves(far_v, states[0][1]))]
    for masks in near:
        last_k += [tuple(swap(x, masks) for x in block) for block in last_k]
    far_kv = [(far_k, far_v)]
    first = [1] + near_q
    states[1] = attend([q_blocks[1]], near_k, [], False)[0]
    states.update(zip(first, attend([q_blocks[i] for i in first], far_kv, [states[i] for i in first], False)))
    rest = far_q[1:]
    if rest:
        blocks = [later(q_blocks[i], 2 * DH, states[1][1]) for i in rest]
        states.update(zip(rest, attend(blocks, near_k + far_kv, [], False)))
    aside = [i for i in far_q if i & top_bit]
    parts = {}
    for group, split in ((aside, False), ([i for i in range(n_q) if i not in aside], False)):
        if group:
            done = attend(
                [q_blocks[i] for i in group], last_k[1:], [states[i] for i in group], True, split
            )
            parts.update(zip(group, done))

    def masks_of(index):
        return tuple(sum(bit for i, bit in enumerate(bits) if index >> i & 1) for bits in q_bits)

    own = [parts[0][0]] + [swap(parts[i][0], masks_of(i)) for i in range(1, n_q)]
    cross = []
    for i in range(1, top_bit):
        beside = [swap(x, masks_of(top_bit)) for x in parts[i | top_bit][1:]]
        merged = pl.pallas_call(
            merge_kernel, out_shape=part_shapes(rows, 1), compiler_params=params(8)
        )(parts[i][1], *beside)
        cross.append([swap(x, masks_of(i), True) for x in merged])
    for i in (top_bit, 0):
        cross.append((swap(parts[i][1], masks_of(i), True),))
    got = iter(landed([own[i] for i in far_q] + [x for part in cross[:-2] for x in part]))
    own = [next(got) if i in far_q else x for i, x in enumerate(own)]
    cross = [[next(got) for _ in part] for part in cross[:-2]] + cross[-2:]
    counts = [1] * n_q + [len(part) for part in cross]
    return tuple(
        pl.pallas_call(
            functools.partial(finish_kernel, n_q, counts),
            out_shape=[f32(rows, width)] * 2,
            in_specs=[smem] + [vmem] * sum(counts),
            compiler_params=params(8),
        )(core, *own, *(x for part in cross for x in part))
    )


def solution(mesh):
    spec = P(AXES, None)
    body = functools.partial(per_device, mesh.shape["pb"], mesh.shape["kv"])
    return jax.shard_map(body, mesh=mesh, in_specs=(spec,) * 6, out_specs=(spec,) * 2, check_vma=False)
```
